128 devices in a mesh: row: 8 (over x_hi, y), col: 16 (over z, x_lo, core).
Axes of the slice: x: 4 (x_hi: 2, x_lo: 2; x = x_hi * 2 + x_lo), y: 4, z: 4, core: 2. Of those that a mesh axis runs over, the one named last changes fastest.
Arguments:
- embeds: bfloat16 [2, 192, 16384], P(None, None, 'col'), may hold values from -40 to 40
- attn_gain: bfloat16 [16384], P('col'), may hold values from 0.099609375 to 1.8984375
- ffn_gain: bfloat16 [16384], P('col'), may hold values from 0.099609375 to 1.8984375
- query_weight: bfloat16 [16384, 16384], P(None, ('row', 'col')), may hold values from -0.046875 to 0.046875
- key_matrix: bfloat16 [16384, 1024], P(None, ('row', 'col')), may hold values from -0.046875 to 0.046875
- value_matrix: bfloat16 [16384, 1024], P(None, ('row', 'col')), may hold values from -0.046875 to 0.046875
- output_weight: bfloat16 [16384, 16384], P(('row', 'col')), may hold values from -0.046875 to 0.046875
- gate_weight: bfloat16 [16384, 13312], P(None, ('row', 'col')), may hold values from -0.046875 to 0.046875
- up_weight: bfloat16 [16384, 13312], P(None, ('row', 'col')), may hold values from -0.046875 to 0.046875
- down_weight: bfloat16 [13312, 16384], P(('row', 'col')), may hold values from -0.0546875 to 0.0546875
- rotated_key_cache: bfloat16 [192, 8, 1024, 128], P('col', 'row'), may hold values from -400 to 400
- stored_value_cache: bfloat16 [192, 8, 1024, 128], P('col', 'row'), may hold values from -6 to 6
- lengths: int32 [192], P('col'), may hold values from 2 to 1024, as said below
- positions: int32 [192], P('col'), may hold values from 0 to 8191
Outputs:
- layer_out: bfloat16 [2, 192, 16384], P(None, None, 'col')
- appended: bfloat16 [2, 192, 2, 1024], P(None, 'col', None, 'row')
The draws below stay inside these ranges and needn't reach their ends.
Inputs may be any that keep to these rules, and one draw needn't show every extreme that they name: `lengths`: every draw has a row with all 1024 slots filled and a row with 2.
All inputs are finite; a program needn't handle non-finite values.
Results may differ from the reference program's by a relative error of at most 0.0075.
Values may be sent and summed in bfloat16 or wider, within the bound.
A program may use at most 192 MiB of HBM per device.

```python
import math
import jax
import jax.numpy as jnp
from jax import lax

MODEL_WIDTH = 16384
QUERY_HEADS = 128
KEY_HEADS = 8
HEAD_WIDTH = 128
FF = 13312
STEPS = 2
CACHE_SLOTS = 1024
BATCH_ROWS = 192


def draw_embeds(key, part):
    key = jax.random.fold_in(key, 11)
    first_key, second_random_key = jax.random.split(key, 2)
    column = jnp.arange(MODEL_WIDTH, dtype=jnp.float32) / MODEL_WIDTH
    row_scale = jnp.exp(jax.random.uniform(second_random_key, (STEPS, BATCH_ROWS, 1), jnp.float32, jnp.log(0.3), jnp.log(3.0)))
    base = jnp.clip(jax.random.normal(first_key, (STEPS, BATCH_ROWS, MODEL_WIDTH), jnp.float32), -6.0, 6.0)
    slope = jnp.exp(0.5 * jnp.log(3.0) * column)
    value_tensor = base * slope * row_scale
    return value_tensor.astype(jnp.bfloat16)


def draw_rotated_key_cache(key, part):
    key = jax.random.fold_in(key, 23)
    first_key = jax.random.fold_in(key, 0)
    tensor_shape = (BATCH_ROWS, KEY_HEADS, CACHE_SLOTS, HEAD_WIDTH)
    value_tensor = 2.5 * jnp.clip(jax.random.normal(first_key, tensor_shape, jnp.float32), -6.0, 6.0)
    return value_tensor.astype(jnp.bfloat16)


def draw_lengths(key, part):
    key = jax.random.fold_in(key, 37)
    first_key, second_random_key = jax.random.split(key)
    value_tensor = jax.random.randint(first_key, (BATCH_ROWS,), 2, CACHE_SLOTS + 1)
    order = jax.random.permutation(second_random_key, BATCH_ROWS)
    value_tensor = value_tensor.at[order[0]].set(CACHE_SLOTS).at[order[1]].set(2)
    return value_tensor.astype(jnp.int32)


def set_ends(array, own_key, smallest, high):
    longest = array.shape.index(max(array.shape))
    spots = []
    for shift in (0, 1):
        where = [jax.random.randint(jax.random.fold_in(own_key, axis), (), 0, length) for axis, length in enumerate(array.shape)]
        where[longest] = (where[longest] + shift) % array.shape[longest]
        spots.append(tuple(where))
    return array.at[spots[0]].set(smallest).at[spots[1]].set(high)


def shard_levels(stream_key, extent, cuts, smallest, high):
    loudness, own = 1.0, jax.random.fold_in(stream_key, 6)
    for position, blocks in cuts:
        draws = jnp.exp(jax.random.uniform(jax.random.fold_in(own, position), (blocks,), jnp.float32, smallest / len(cuts), high / len(cuts)))
        loudness = loudness * jnp.repeat(draws, extent[position] // blocks).reshape([-1 if axis == position else 1 for axis in range(len(extent))])
    return loudness


def gaussian(rng, shape, deviation, reach, shards=(), held_as=jnp.bfloat16):
    entries = deviation * jax.random.normal(rng, shape, jnp.float32)
    if shards:
        entries = entries * shard_levels(rng, shape, shards, -0.22, 0.18)
    return jnp.clip(entries, -reach, reach).astype(held_as)


def setup_inputs(seed: int = 0) -> dict:
    seeds = jax.random.split(jax.random.key(seed), 15)
    embeds = draw_embeds(jax.random.fold_in(seeds[14], 71), 0)
    attn_gain = jnp.clip(1.0 + 0.18 * jax.random.normal(seeds[1], (MODEL_WIDTH,), jnp.float32), 0.099609375, 1.8984375).astype(jnp.bfloat16)
    ffn_gain = jnp.clip(1.0 + 0.18 * jax.random.normal(seeds[2], (MODEL_WIDTH,), jnp.float32), 0.099609375, 1.8984375).astype(jnp.bfloat16)
    query_weight = gaussian(seeds[3], (MODEL_WIDTH, QUERY_HEADS * HEAD_WIDTH), MODEL_WIDTH ** -0.5, 0.046875, ((1, 128),))
    key_matrix = gaussian(seeds[4], (MODEL_WIDTH, KEY_HEADS * HEAD_WIDTH), MODEL_WIDTH ** -0.5, 0.046875, ((1, 128),))
    value_matrix = gaussian(seeds[5], (MODEL_WIDTH, KEY_HEADS * HEAD_WIDTH), MODEL_WIDTH ** -0.5, 0.046875, ((1, 128),))
    output_weight = gaussian(seeds[6], (QUERY_HEADS * HEAD_WIDTH, MODEL_WIDTH), (QUERY_HEADS * HEAD_WIDTH) ** -0.5, 0.046875, ((0, 128),))
    gate_weight = gaussian(seeds[7], (MODEL_WIDTH, FF), MODEL_WIDTH ** -0.5, 0.046875, ((1, 128),))
    up_weight = gaussian(seeds[8], (MODEL_WIDTH, FF), MODEL_WIDTH ** -0.5, 0.046875, ((1, 128),))
    down_weight = gaussian(seeds[9], (FF, MODEL_WIDTH), FF ** -0.5, 0.0546875, ((0, 128),))
    rotated_key_cache = draw_rotated_key_cache(jax.random.fold_in(seeds[14], 71), 0)
    stored_value_cache = gaussian(seeds[11], (BATCH_ROWS, KEY_HEADS, CACHE_SLOTS, HEAD_WIDTH), 1.0, 6.0, ((0, 16), (1, 8)))
    lengths = draw_lengths(jax.random.fold_in(seeds[14], 71), 0)
    positions = set_ends(jax.random.randint(seeds[13], (BATCH_ROWS,), 0, 8192), jax.random.fold_in(seeds[13], 1), 0, 8191).astype(jnp.int32)
    return dict(embeds=embeds, attn_gain=attn_gain, ffn_gain=ffn_gain, query_weight=query_weight, key_matrix=key_matrix, value_matrix=value_matrix, output_weight=output_weight, gate_weight=gate_weight, up_weight=up_weight, down_weight=down_weight, rotated_key_cache=rotated_key_cache, stored_value_cache=stored_value_cache, lengths=lengths, positions=positions)


EPS = 1e-05
THETA = 500000.0

def rope_tables(positions, head_size):
    half_size = head_size // 2
    frequency = THETA ** (-2.0 * jnp.arange(half_size, dtype=jnp.float32) / head_size)
    angles = positions.astype(jnp.float32)[:, None] * frequency[None, :]
    return (jnp.cos(angles), jnp.sin(angles))

def apply_rotation(value_tensor, cosine_table, sine_table):
    half_size = value_tensor.shape[-1] // 2
    leading = value_tensor[..., :half_size]
    trailing = value_tensor[..., half_size:]
    cosine_table = cosine_table[:, None, :]
    sine_table = sine_table[:, None, :]
    return jnp.concatenate([leading * cosine_table - trailing * sine_table, trailing * cosine_table + leading * sine_table], axis=-1)

def rms_scale(value_tensor, gain):
    widened = value_tensor.astype(jnp.float32)
    mean_square = lax.optimization_barrier(jnp.mean(widened * widened, axis=-1, keepdims=True))
    return (widened * lax.rsqrt(mean_square + EPS) * gain.astype(jnp.float32)).astype(jnp.bfloat16)

def attend_cache(query_tensor, rotated_key_cache, stored_value_cache, valid_mask, new_keys, new_values):
    factor = 1.0 / math.sqrt(query_tensor.shape[-1])
    cached = jnp.einsum('bgqd,bgjd->bgqj', query_tensor.astype(jnp.float32), rotated_key_cache.astype(jnp.float32)) * factor
    recent = jnp.einsum('bgqd,bgtd->bgqt', query_tensor.astype(jnp.float32), new_keys.astype(jnp.float32)) * factor
    usable = valid_mask[:, None, None, :]
    highest = jnp.maximum(lax.optimization_barrier(jnp.max(jnp.where(usable, cached, -jnp.inf), axis=-1)), lax.optimization_barrier(jnp.max(recent, axis=-1)))[..., None]
    cached_weight = jnp.where(usable, jnp.exp(cached - highest), 0.0)
    recent_weight = jnp.exp(recent - highest)
    denominator = lax.optimization_barrier(jnp.sum(cached_weight, axis=-1, keepdims=True)) + lax.optimization_barrier(jnp.sum(recent_weight, axis=-1, keepdims=True))
    cached_prob = (cached_weight / denominator).astype(jnp.bfloat16)
    recent_prob = (recent_weight / denominator).astype(jnp.bfloat16)
    blended = jnp.einsum('bgqj,bgjd->bgqd', cached_prob.astype(jnp.float32), stored_value_cache.astype(jnp.float32))
    blended = blended + jnp.einsum('bgqt,bgtd->bgqd', recent_prob.astype(jnp.float32), new_values.astype(jnp.float32))
    return blended.astype(jnp.bfloat16)

def reference(embeds, attn_gain, ffn_gain, query_weight, key_matrix, value_matrix, output_weight, gate_weight, up_weight, down_weight, rotated_key_cache, stored_value_cache, lengths, positions):
    batch_count = embeds.shape[1]
    queries_per_group = QUERY_HEADS // KEY_HEADS
    valid_mask = jnp.arange(CACHE_SLOTS, dtype=jnp.int32)[None, :] < lengths[:, None]
    latest_keys = []
    latest_values = []
    outputs = []
    appended = []
    for step in range(STEPS):
        current = embeds[step]
        normed = rms_scale(current, attn_gain)
        query_tensor = jnp.dot(normed, query_weight, preferred_element_type=jnp.float32)
        key_tensor = jnp.dot(normed, key_matrix, preferred_element_type=jnp.float32)
        value_tensor = jnp.dot(normed, value_matrix, preferred_element_type=jnp.float32)
        cosine_table, sine_table = rope_tables(positions + step, HEAD_WIDTH)
        query_tensor = apply_rotation(query_tensor.reshape(batch_count, QUERY_HEADS, HEAD_WIDTH), cosine_table, sine_table).astype(jnp.bfloat16)
        key_tensor = apply_rotation(key_tensor.reshape(batch_count, KEY_HEADS, HEAD_WIDTH), cosine_table, sine_table).astype(jnp.bfloat16)
        value_tensor = value_tensor.reshape(batch_count, KEY_HEADS, HEAD_WIDTH).astype(jnp.bfloat16)
        latest_keys.append(key_tensor)
        latest_values.append(value_tensor)
        appended.append(jnp.stack([key_tensor.reshape(batch_count, KEY_HEADS * HEAD_WIDTH), value_tensor.reshape(batch_count, KEY_HEADS * HEAD_WIDTH)], axis=1))
        head_count = attend_cache(query_tensor.reshape(batch_count, KEY_HEADS, queries_per_group, HEAD_WIDTH), rotated_key_cache, stored_value_cache, valid_mask, jnp.stack(latest_keys, axis=2), jnp.stack(latest_values, axis=2))
        head_count = head_count.reshape(batch_count, QUERY_HEADS * HEAD_WIDTH)
        residual = (current.astype(jnp.float32) + jnp.dot(head_count, output_weight, preferred_element_type=jnp.float32)).astype(jnp.bfloat16)
        normed_ffn = rms_scale(residual, ffn_gain)
        gate = jnp.dot(normed_ffn, gate_weight, preferred_element_type=jnp.float32)
        upper = jnp.dot(normed_ffn, up_weight, preferred_element_type=jnp.float32)
        hidden = (jax.nn.silu(gate) * upper).astype(jnp.bfloat16)
        result = residual.astype(jnp.float32) + jnp.dot(hidden, down_weight, preferred_element_type=jnp.float32)
        outputs.append(result.astype(jnp.bfloat16))
    return (jnp.stack(outputs), jnp.stack(appended))
```

```python
import functools

import jax
import jax.numpy as jnp
from jax import lax
from jax.experimental import pallas as pl
from jax.experimental.pallas import tpu as pltpu
from jax.sharding import PartitionSpec as P

WIDTH = 16384
HEAD = 128
STEPS = 2
SLOTS = 1024
EPS = 1e-05
THETA = 500000.0
ROWS = 192
LOCAL = 12
FFL = 104
BF = jnp.bfloat16
F32 = jnp.float32
MESH = pl.DeviceIdType.MESH
ORDERS = (("x", "y", "z"), ("y", "z", "x"), ("z", "x", "y"))
NT = (((1,), (1,)), ((), ()))


def coords():
    row = lax.axis_index("row")
    col = lax.axis_index("col")
    return dict(x=(row // 4) * 2 + (col // 2) % 2, y=row % 4, z=col // 4, k=col % 2)


def device(c):
    return {"row": (c["x"] // 2) * 4 + c["y"], "col": c["z"] * 4 + (c["x"] % 2) * 2 + c["k"]}


def moved(c, d, s):
    e = dict(c)
    e[d] = (c[d] + s + 4) % 4
    return e


def remote(src, dst, ss, rs, target):
    return pltpu.make_async_remote_copy(
        src_ref=src, dst_ref=dst, send_sem=ss, recv_sem=rs, device_id=target, device_id_type=MESH
    )


def width_of(full):
    return 1024 if "x" in full else 512


def block(ref, t, c, full, d, q, half=None):
    pos = dict(c)
    pos[d] = q
    z = slice(None) if "z" in full else pos["z"]
    y = slice(None) if "y" in full else pos["y"]
    w = width_of(full)
    if "x" in full:
        xl, base = slice(None), 0
    else:
        xl, base = pos["x"] % 2, (pos["x"] // 2) * 512
    if half is not None:
        w = w // 2
        base = base + half * w
    if not isinstance(base, int):
        base = pl.multiple_of(base, 256)
    return ref.at[z, xl, y, t, :, pl.ds(base, w)]


def lead_shape(full):
    return ((4,) if "z" in full else ()) + ((2,) if "x" in full else ()) + ((4,) if "y" in full else ())


def lead_index(shape, n):
    idx = []
    for size in reversed(shape):
        idx.append(n % size)
        n = n // size
    return tuple(reversed(idx))


def for_pieces(shape, body):
    total = 1
    for size in shape:
        total *= size
    if total == 1:
        body(())
    else:

        def step(n, carry):
            body(lead_index(shape, n))
            return carry

        lax.fori_loop(0, total, step, 0)


WAYS = ((0, 1), (1, -1))


def counted(ref, n):
    return {9: ref.at[0, 0, pl.ds(0, 3), :, :, pl.ds(0, 512)], 36: ref.at[0, :, pl.ds(0, 3)]}.get(
        n, ref.at[pl.ds(0, n // 48)]
    )


def wait_sent(ref, n, sem):
    part = counted(ref, n)
    pltpu.make_async_copy(part, part, sem).wait()


def gather(g, c, ss, rs):
    def send(src, d, s, ph, sem):
        remote(src, src, ss.at[ph], rs.at[sem], device(moved(c, d, s))).start()

    for ph in range(2):
        for o in (1, 3, 2):
            for t in range(3):
                d = ORDERS[t][ph]
                send(block(g, t, c, ORDERS[t][:ph], d, c[d]), d, o, ph, ph)
        yield
        wait_sent(g, 9 * 4**ph, rs.at[ph])
    axes = [(t, ORDERS[t][2], ORDERS[t][:2]) for t in range(3)]
    for part in (0, 1):
        for t, d, full in axes:
            for i, s in WAYS:
                h = i if part == 0 else 1 - i
                send(block(g, t, c, full, d, c[d], h), d, s, 2, 3 + 2 * t + i if part == 0 else 2)
    yield
    for t, d, full in axes:
        for i, s in WAYS:
            h = block(g, t, c, full, d, (c[d] - s + 4) % 4, i)
            pltpu.make_async_copy(h, h, rs.at[3 + 2 * t + i]).wait()
            send(h, d, s, 2, 2)
    yield
    wait_sent(g, 96, rs.at[2])
    for ph in range(3):
        wait_sent(g, (9, 36, 144)[ph], ss.at[ph])


def scatter(p, fwd, land, c, ss, rs):
    def send(src, dst, d, s, st, sem):
        remote(src, dst, ss.at[st], rs.at[sem], device(moved(c, d, s))).start()

    axes = [(t, ORDERS[t][2], ORDERS[t][:2]) for t in range(3)]

    def half(t, i, full, h):
        w = width_of(full) // 2
        lead = (slice(None),) * len(lead_shape(full))
        return land[t][0].at[(i,) + lead + (slice(None), pl.ds(h * w, w))]

    for t, d, full in axes:
        for i, s in WAYS:
            send(block(p, t, c, full, d, (c[d] + 2) % 4, i), fwd[t].at[i], d, s, 0, 3 + 2 * t + i)
    for t, d, full in axes:
        for i, s in WAYS:
            send(block(p, t, c, full, d, (c[d] + s + 4) % 4, 1 - i), half(t, i, full, 1 - i), d, s, 0, 0)
    yield
    for t, d, full in axes:
        for i, s in WAYS:
            f = fwd[t].at[i]
            pltpu.make_async_copy(f, f, rs.at[3 + 2 * t + i]).wait()
            mine = block(p, t, c, full, d, (c[d] + s + 4) % 4, i)

            def add(idx, mine=mine, t=t, i=i):
                a = mine[idx].astype(F32) + fwd[t][(i,) + idx].astype(F32)
                mine[idx] = a.astype(BF)

            for_pieces(lead_shape(full), add)
            send(mine, half(t, i, full, i), d, s, 0, 0)
    yield
    wait_sent(p, 96, rs.at[0])
    for t, d, full in axes:
        mine = block(p, t, c, full, d, c[d])

        def total(idx, mine=mine, t=t):
            a = mine[idx].astype(F32) + (land[t][0][(0,) + idx].astype(F32) + land[t][0][(1,) + idx].astype(F32))
            mine[idx] = a.astype(BF)

        for_pieces(lead_shape(full), total)
    for st in (1, 2):
        axes = [(t, ORDERS[t][2 - st], ORDERS[t][: 2 - st]) for t in range(3)]
        for o in (1, 3, 2):
            for t, d, full in axes:
                send(block(p, t, c, full, d, (c[d] + o) % 4), land[t][st].at[o - 1], d, o, st, st)
        yield
        wait_sent(p, 36 // 4 ** (st - 1), rs.at[st])
        for t, d, full in axes:
            mine = block(p, t, c, full, d, c[d])

            def total(idx, mine=mine, t=t, st=st):
                a = mine[idx].astype(F32)
                for o in range(3):
                    a = a + land[t][st][(o,) + idx].astype(F32)
                mine[idx] = a.astype(BF)

            for_pieces(lead_shape(full), total)
    for st in range(3):
        wait_sent(p, (144, 36, 9)[st], ss.at[st])


def iota(shape, d):
    return lax.broadcasted_iota(jnp.int32, shape, d)


def onehot(cond):
    return jnp.where(cond, 1.0, 0.0).astype(BF)


def mm(a, b):
    return jnp.dot(a, b, preferred_element_type=F32)


def mm_nt(a, b):
    return lax.dot_general(a, b, NT, preferred_element_type=F32)


def kernel(*refs):
    names = (
        "emb_h", "attn_gain", "ffn_gain", "wq_h", "kh_h", "vh_h", "wo_h", "g_h", "u_h", "wd_h", "kc_h", "vc_h", "lens",
        "pos", "freq", "out", "app", "g", "p", "emb", "wq", "kv", "wo", "gate", "up", "wd", "kc", "vc", "ginv",
        "acc", "ssq", "qs", "qr", "kn", "vn", "qb", "sbuf", "pb", "ho", "hr", "xs", "xr", "res", "fin", "to_rows",
        "to_tokens", "by_row", "by_head", "spread", "place", "load_sem", "load_out", "pair_s", "pair_r", "ag_s",
        "ag_r", "rs_s", "rs_r", "a2a_s", "a2a_r", "gi_s", "gi_r", "x_s", "x_r", "f_s", "f_r",
    )
    n = dict(zip(names, refs[: len(names)]))
    rest = refs[len(names) :]
    r = type("Refs", (), n)
    c = coords()
    k = c["k"]
    col = lax.axis_index("col")
    row = lax.axis_index("row")
    xl, xh, y, z = c["x"] % 2, c["x"] // 2, c["y"], c["z"]
    mate = {"row": row, "col": col + 1 - 2 * k}
    far = dict(c)
    far["x"] = (c["x"] + 2) % 4

    def peer(o):
        return {"row": row, "col": (col + o) % 16}

    loads = {}

    def load(name, i, src, dst):
        cp = pltpu.make_async_copy(src, dst, r.load_sem.at[i])
        cp.start()
        loads[name] = cp

    load("emb", 0, r.emb_h, r.emb)

    bar = pltpu.get_barrier_semaphore()
    greet = [peer(o) for o in range(1, 16)]
    greet += [device(moved(c, "y", 1)), device(moved(c, "y", 2)), device(moved(c, "y", 3)), device(far)]
    other = dict(c)
    other["x"] = (c["x"] + 3 - 2 * (c["x"] % 2)) % 4
    greet.append(device(other))
    for target in greet:
        pl.semaphore_signal(bar, inc=1, device_id=target, device_id_type=MESH)
    pl.semaphore_wait(bar, len(greet))

    pair = {}

    def share(i, src_of, dst, blocks):
        for b in blocks:
            remote(src_of(1 - k, b), dst.at[(k,) + b], r.pair_s.at[i], r.pair_r.at[i], mate).start()
            pltpu.make_async_copy(src_of(k, b), dst.at[(k,) + b], r.load_sem.at[i]).start()

    def share_wait(i, dst):
        pltpu.make_async_copy(dst.at[k], dst.at[k], r.load_sem.at[i]).wait()
        whole = remote(dst.at[k], dst.at[1 - k], r.pair_s.at[i], r.pair_r.at[i], mate)
        whole.wait_recv()
        pair[i] = whole

    def lanes(ref):
        return lambda par, b: ref.at[:, pl.ds(pl.multiple_of((2 * b[0] + par) * 1024, 1024), 1024)]

    eight = [(b,) for b in range(8)]

    ga = r.attn_gain[...].astype(F32).reshape(1, 1024)
    gf = r.ffn_gain[...].astype(F32).reshape(1, 1024)
    r.ginv[z * 2 + xl] = jnp.where(iota((8, 1024), 0) == 0, 1.0 / (ga * ga), 1.0 / (gf * gf))

    def own(ref, t):
        return block(ref, t, c, (), "z", z)

    loads["emb"].wait()
    gain_a = jnp.where(xh == 0, ga[:, :512], ga[:, 512:])
    gain_f = jnp.where(xh == 0, gf[:, :512], gf[:, 512:])

    def emb_piece(s, t):
        return r.emb[s, y, t, :, pl.ds(pl.multiple_of(xh * 512, 512), 512)].astype(F32)

    def startup():
        for o in range(1, 8):
            dst = r.ginv.at[z * 2 + xl]
            remote(dst, dst, r.gi_s.at[0], r.gi_r.at[0], peer(2 * o)).start()
        share(1, lambda par, b: r.wq_h.at[:, par], r.wq, [()])
        share(2, lanes(r.kh_h), r.kv.at[0], eight)
        share(9, lanes(r.vh_h), r.kv.at[1], eight)
        load("kc", 7, r.kc_h, r.kc)
        load("vc", 8, r.vc_h, r.vc)
        share(3, lanes(r.wo_h), r.wo, eight)
        share(4, lanes(r.g_h), r.gate, eight)
        share(5, lanes(r.u_h), r.up, eight)
        share(6, lanes(r.wd_h), r.wd, eight)
        a, b = iota((256, ROWS), 0), iota((256, ROWS), 1)
        r.to_rows[...] = onehot(((a & 15) < LOCAL) & (b == (a >> 4) * LOCAL + (a & 15)))
        a, b = iota((ROWS, 256), 0), iota((ROWS, 256), 1)
        r.to_tokens[...] = onehot(((b & 15) < LOCAL) & (a == (b >> 4) * LOCAL + (b & 15)))
        r.by_row[...] = onehot(((a >> 4) == (b & 15)) & ((a & 15) == (b >> 4)))
        a, b = iota((256, ROWS), 0), iota((256, ROWS), 1)
        r.by_head[...] = onehot(((b >> 4) == (a & 15)) & ((b & 15) == (a >> 4)))
        a, b = iota((ROWS, 16), 0), iota((ROWS, 16), 1)
        r.spread[...] = onehot((a >> 4) == b)
        a, b = iota((128, 256), 0), iota((128, 256), 1)
        for src in range(16):
            head_col = (a >> 4) * 8 + (a & 7) + (src // 2) * 16 + ((a >> 3) & 1) * 128
            r.place[src] = onehot((a < 32) & (b == head_col))

    first = {"w": True}

    def squares(s, g, zz, xx, which):
        v = g[zz, xx].reshape(ROWS, 1024)
        gi_row = r.ginv[zz * 2 + xx, pl.ds(which, 1), :]
        acc = jnp.zeros((ROWS, 128), F32)
        for j in range(8):
            w = v[:, j * 128 : (j + 1) * 128].astype(F32)
            acc = acc + w * w * gi_row[:, j * 128 : (j + 1) * 128]
        r.ssq[s] += acc

    def stream(s):
        sends = []
        g, p = r.g.at[s], r.p.at[s]
        fwd = [rest[t * 4].at[s] for t in range(3)]
        land = [[rest[t * 4 + 1 + st].at[s] for st in range(3)] for t in range(3)]
        for t in range(3):
            own(g, t)[...] = (emb_piece(s, t) * gain_a).astype(BF)
        it = gather(g, c, r.ag_s.at[s], r.ag_r.at[s])
        next(it)
        if s == 0:
            startup()
        yield
        yield from it

        if first.pop("w", False):
            share_wait(1, r.wq)
            share_wait(2, r.kv.at[0])
            share_wait(9, r.kv.at[1])
            part = r.ginv.at[pl.ds(0, 7)]
            pltpu.make_async_copy(part, part, r.gi_r.at[0]).wait()
        r.acc[s] = jnp.zeros((3, ROWS, 128), F32)
        r.ssq[s] = jnp.zeros((ROWS, 128), F32)

        def qkv(i, carry):
            zz, xx = i // 2, i % 2
            v = g[zz, xx].reshape(ROWS, 1024)
            wq = jnp.concatenate([r.wq[0, i], r.wq[1, i]], axis=1)
            q = mm(v, wq)
            r.acc[s, 0] += q[:, :128]
            r.acc[s, 1] += q[:, 128:]
            wkv = [r.kv[j, core, i].astype(F32) for core in range(2) for j in range(2)]
            wkv = jnp.concatenate(wkv, axis=0).astype(BF)
            r.acc[s, 2, :, pl.ds(0, 32)] += mm_nt(v, wkv)
            squares(s, g, zz, xx, 0)
            return carry

        lax.fori_loop(0, 4, qkv, 0)
        yield
        lax.fori_loop(4, 8, qkv, 0)
        total = jnp.sum(r.ssq[s], axis=-1, keepdims=True)
        high = total.astype(BF).astype(F32)
        low = total - high
        lane = iota((ROWS, 128), 1)
        tail = jnp.where(lane == 32, high, jnp.where(lane == 33, low, r.acc[s, 2]))
        sums = jnp.concatenate([r.acc[s, 0], r.acc[s, 1], tail], axis=1).astype(BF)
        r.qs[s] = mm(r.to_rows[...], sums).astype(BF).reshape(16, 16, 384)
        for o in range(1, 16):
            remote(r.qs.at[s, (col + o) % 16], r.qr.at[s, col], r.a2a_s.at[s, 0], r.a2a_r.at[s, 0], peer(o)).start()
        r.qr[s, col] = r.qs[s, col]
        yield
        part = r.qr.at[s, pl.ds(0, 15)]
        pltpu.make_async_copy(part, part, r.a2a_r.at[s, 0]).wait()

        ends = r.qr[s, 0, :, pl.ds(256, 128)].astype(F32) + r.qr[s, 1, :, pl.ds(256, 128)].astype(F32)
        l16 = iota((16, 128), 1)
        square = jnp.sum(jnp.where((l16 == 32) | (l16 == 33), ends, 0.0), axis=-1, keepdims=True)
        scale = lax.rsqrt(square / WIDTH + EPS)
        angle = jnp.zeros((16, 128), jnp.int32)
        for j in range(LOCAL):
            angle = jnp.where(iota((16, 128), 0) == j, r.pos[j] + s, angle)
        angle = angle.astype(F32) * r.freq[...]
        cos, sin = jnp.cos(angle), jnp.sin(angle)
        sin = jnp.where(l16 < 64, -sin, sin)

        def rotate(v):
            return (v * cos + pltpu.roll(v, 64, 1) * sin).astype(BF)

        heads = []
        for h in range(8):
            both = r.qr[s, 2 * h, :, pl.ds(0, 256)].astype(F32) + r.qr[s, 2 * h + 1, :, pl.ds(0, 256)].astype(F32)
            both = both * scale
            heads += [rotate(both[:, :128]), rotate(both[:, 128:])]
        q_all = mm(r.by_row[...], jnp.concatenate(heads, axis=0)).astype(BF)
        r.qb[s] = q_all
        kv = mm(r.qr[s, 0, :, pl.ds(256, 128)], r.place[0])
        for src in range(1, 16):
            kv = kv + mm(r.qr[s, src, :, pl.ds(256, 128)], r.place[src])
        kv = kv * scale
        r.kn[s] = rotate(kv[:, :128])
        r.vn[s] = kv[:, 128:].astype(BF)
        r.app[s, 0] = r.kn[s]
        r.app[s, 1] = r.vn[s]

        if s == 0:
            loads["kc"].wait()
            loads["vc"].wait()
        factor = 1.0 / (HEAD**0.5)
        slot = iota((16, SLOTS), 1)
        qf = r.qb[s].astype(F32)
        fresh = []
        top = None
        for s2 in range(s + 1):
            sc = jnp.sum(qf * mm(r.spread[...], r.kn[s2]), axis=-1, keepdims=True) * factor
            fresh.append(sc)
            top = sc if top is None else jnp.maximum(top, sc)
        for j in range(LOCAL):
            sc = mm_nt(r.qb[s, pl.ds(j * 16, 16), :], r.kc[j]) * factor
            r.sbuf[pl.ds(j * 16, 16), :] = jnp.where(slot < r.lens[j], sc, -1e30)
        dens = []
        tops = []
        for j in range(LOCAL):
            sc = r.sbuf[pl.ds(j * 16, 16), :]
            m = jnp.maximum(jnp.max(sc, axis=-1, keepdims=True), top[j * 16 : j * 16 + 16])
            w = jnp.exp(sc - m)
            r.pb[pl.ds(j * 16, 16), :] = w.astype(BF)
            dens.append(jnp.sum(w, axis=-1, keepdims=True))
            tops.append(m)
        den = jnp.concatenate(dens, axis=0)
        m = jnp.concatenate(tops, axis=0)
        o = jnp.concatenate([mm(r.pb[pl.ds(j * 16, 16), :], r.vc[j]) for j in range(LOCAL)], axis=0)
        for s2 in range(s + 1):
            w = jnp.exp(fresh[s2] - m)
            den = den + w
            o = o + w.astype(BF).astype(F32) * mm(r.spread[...], r.vn[s2])
        o = (o / den).astype(BF)
        ho = mm(r.by_head[...], o).astype(BF).reshape(8, 2, 16, 128)
        for h in range(8):
            r.ho[s, h] = jnp.concatenate([ho[h, 0], ho[h, 1]], axis=1)
        for o_ in range(1, 16):
            remote(
                r.ho.at[s, ((col + o_) % 16) // 2], r.hr.at[s, col], r.a2a_s.at[s, 1], r.a2a_r.at[s, 1], peer(o_)
            ).start()
        r.hr[s, col] = r.ho[s, col // 2]
        yield
        if s == 0:
            share_wait(3, r.wo)
        part = r.hr.at[s, pl.ds(0, 15)]
        pltpu.make_async_copy(part, part, r.a2a_r.at[s, 1]).wait()

        attn = mm(r.to_tokens[...], r.hr[s].reshape(256, 256)).astype(BF)

        def project(i, carry):
            w = jnp.concatenate([r.wo[0, i], r.wo[1, i]], axis=0)
            p[i // 2, i % 2] = mm(attn, w).astype(BF).reshape(4, 3, 16, 1024)
            return carry

        lax.fori_loop(0, 8, project, 0)
        yield from scatter(p, fwd, land, c, r.rs_s.at[s], r.rs_r.at[s])
        for t in range(3):
            v = (emb_piece(s, t) + own(p, t)[...].astype(F32)).astype(BF)
            r.res[s, t] = v
            own(g, t)[...] = (v.astype(F32) * gain_f).astype(BF)
        yield from gather(g, c, r.ag_s.at[s], r.ag_r.at[s])

        if s == 0:
            share_wait(4, r.gate)
            share_wait(5, r.up)
        gap = jnp.zeros((128 - FFL, 1024), BF)
        r.xs[s] = jnp.zeros((4, ROWS, 128), F32)
        r.ssq[s] = jnp.zeros((ROWS, 128), F32)

        def slab(i, carry):
            zz, xx = i // 2, i % 2
            v = g[zz, xx].reshape(ROWS, 1024)
            for core in range(2):
                w = jnp.concatenate([r.gate[core, i], gap, r.up[core, i], gap], axis=0)
                v2 = mm_nt(v, w)
                r.xs[s, core] += v2[:, :128]
                r.xs[s, 2 + core] += v2[:, 128:]
            squares(s, g, zz, xx, 1)
            return carry

        lax.fori_loop(0, 4, slab, 0)
        yield
        lax.fori_loop(4, 8, slab, 0)
        total = jnp.sum(r.ssq[s], axis=-1, keepdims=True)
        r.xs[s, 0] = jnp.where(lane < FFL, r.xs[s, 0], total)
        cp = remote(r.xs.at[s], r.xr.at[s], r.x_s.at[s], r.x_r.at[s], mate)
        cp.start()
        yield
        if s == 0:
            share_wait(6, r.wd)
        cp.wait()
        first_sum = r.xs[s, 0] + r.xr[s, 0]
        square = jnp.sum(jnp.where(lane == FFL, first_sum, 0.0), axis=-1, keepdims=True)
        scale = lax.rsqrt(square / WIDTH + EPS)
        hidden = []
        for core in range(2):
            gate = (first_sum if core == 0 else r.xs[s, core] + r.xr[s, core]) * scale
            up = (r.xs[s, 2 + core] + r.xr[s, 2 + core]) * scale
            act = gate / (1.0 + jnp.exp(-gate)) * up
            hidden.append(jnp.where(lane < FFL, act, 0.0).astype(BF))
        hidden = jnp.concatenate(hidden, axis=1)

        def down(i, carry):
            v = mm(hidden, jnp.concatenate([r.wd[0, i], gap, r.wd[1, i], gap], axis=0))
            p[i // 2, i % 2] = v.astype(BF).reshape(4, 3, 16, 1024)
            return carry

        lax.fori_loop(0, 8, down, 0)
        yield from scatter(p, fwd, land, c, r.rs_s.at[s], r.rs_r.at[s])

        def fpiece(yy, hh):
            return r.fin.at[s, yy, :, :, pl.ds(pl.multiple_of(hh * 512, 512), 512)]

        for t in range(3):
            v = r.res[s, t].astype(F32) + own(p, t)[...].astype(F32)
            r.fin[s, y, t, :, pl.ds(pl.multiple_of(xh * 512, 512), 512)] = v.astype(BF)
        mine = fpiece(y, xh)

        def fsend(piece, target, i):
            cp = remote(piece, piece, r.f_s.at[s, i], r.f_r.at[s, i], target)
            cp.start()
            sends.append(cp)

        def farrive(piece, i):
            remote(piece, piece, r.f_s.at[s, i], r.f_r.at[s, i], mate).wait_recv()

        fsend(mine, device(far), 0)
        for o_ in (1, 3, 2):
            fsend(mine, device(moved(c, "y", o_)), o_)
        yield
        theirs = fpiece(y, 1 - xh)
        farrive(theirs, 0)
        for o_ in (1, 3, 2):
            fsend(theirs, device(moved(c, "y", o_)), 3 + o_)
        yield
        for o_ in (1, 2, 3):
            farrive(fpiece((y + 4 - o_) % 4, xh), o_)
        for o_ in (1, 2, 3):
            farrive(fpiece((y + 4 - o_) % 4, 1 - xh), 3 + o_)
        cp = pltpu.make_async_copy(r.fin.at[s], r.out.at[s], r.load_out.at[s])
        cp.start()
        for e in sends:
            e.wait_send()
        for i, ref in ((0, r.qr), (1, r.hr)):
            part = ref.at[s, pl.ds(0, 15)]
            pltpu.make_async_copy(part, part, r.a2a_s.at[s, i]).wait()
        cp.wait()

    live = [stream(s) for s in range(STEPS)]
    for s in SCHEDULE:
        next(live[int(s)], None)
    for it in live:
        for _ in it:
            pass
    part = r.ginv.at[pl.ds(0, 7)]
    pltpu.make_async_copy(part, part, r.gi_s.at[0]).wait()
    for i in pair:
        pair[i].wait_send()


SCHEDULE = "0101001" + "01" * 22


def rope_frequency(head_size):
    half_size = head_size // 2
    return THETA ** (-2.0 * jnp.arange(half_size, dtype=jnp.float32) / head_size)


def on_device(
    embeds,
    attn_gain,
    ffn_gain,
    query_weight,
    key_matrix,
    value_matrix,
    output_weight,
    gate_weight,
    up_weight,
    down_weight,
    rotated_key_cache,
    stored_value_cache,
    lengths,
    positions,
):
    freq = rope_frequency(HEAD)
    freq = jnp.concatenate([freq, freq]).reshape(1, HEAD)
    anyspace = pl.BlockSpec(memory_space=pl.ANY)
    vmem = pl.BlockSpec(memory_space=pltpu.VMEM)
    smem = pl.BlockSpec(memory_space=pltpu.SMEM)
    scratch = [
        pltpu.VMEM((2, 4, 2, 4, 3, 16, 1024), BF),
        pltpu.VMEM((2, 4, 2, 4, 3, 16, 1024), BF),
        pltpu.VMEM((2, 4, 3, 16, 1024), BF),
        pltpu.VMEM((2, 8, 1024, 128), BF),
        pltpu.VMEM((2, 2, 8, 8, 1024), BF),
        pltpu.VMEM((2, 8, 128, 1024), BF),
        pltpu.VMEM((2, 8, FFL, 1024), BF),
        pltpu.VMEM((2, 8, FFL, 1024), BF),
        pltpu.VMEM((2, 8, FFL, 1024), BF),
        pltpu.VMEM((LOCAL, SLOTS, HEAD), BF),
        pltpu.VMEM((LOCAL, SLOTS, HEAD), BF),
        pltpu.VMEM((8, 8, 1024), F32),
        pltpu.VMEM((2, 3, ROWS, 128), F32),
        pltpu.VMEM((2, ROWS, 128), F32),
        pltpu.VMEM((2, 16, 16, 384), BF),
        pltpu.VMEM((2, 16, 16, 384), BF),
        pltpu.VMEM((2, 16, 128), BF),
        pltpu.VMEM((2, 16, 128), BF),
        pltpu.VMEM((2, ROWS, 128), BF),
        pltpu.VMEM((ROWS, SLOTS), F32),
        pltpu.VMEM((ROWS, SLOTS), BF),
        pltpu.VMEM((2, 8, 16, 256), BF),
        pltpu.VMEM((2, 16, 16, 256), BF),
        pltpu.VMEM((2, 4, ROWS, 128), F32),
        pltpu.VMEM((2, 4, ROWS, 128), F32),
        pltpu.VMEM((2, 3, 16, 512), BF),
        pltpu.VMEM((2, 4, 3, 16, 1024), BF),
        pltpu.VMEM((256, ROWS), BF),
        pltpu.VMEM((ROWS, 256), BF),
        pltpu.VMEM((ROWS, 256), BF),
        pltpu.VMEM((256, ROWS), BF),
        pltpu.VMEM((ROWS, 16), BF),
        pltpu.VMEM((16, 128, 256), BF),
        pltpu.SemaphoreType.DMA((10,)),
        pltpu.SemaphoreType.DMA((2,)),
        pltpu.SemaphoreType.DMA((10,)),
        pltpu.SemaphoreType.DMA((10,)),
        pltpu.SemaphoreType.DMA((2, 3)),
        pltpu.SemaphoreType.DMA((2, 9)),
        pltpu.SemaphoreType.DMA((2, 3)),
        pltpu.SemaphoreType.DMA((2, 9)),
        pltpu.SemaphoreType.DMA((2, 2)),
        pltpu.SemaphoreType.DMA((2, 2)),
        pltpu.SemaphoreType.DMA((1,)),
        pltpu.SemaphoreType.DMA((1,)),
        pltpu.SemaphoreType.DMA((2,)),
        pltpu.SemaphoreType.DMA((2,)),
        pltpu.SemaphoreType.DMA((2, 7)),
        pltpu.SemaphoreType.DMA((2, 7)),
    ]
    for t in range(3):
        full = ORDERS[t][:2]
        scratch.append(pltpu.VMEM((2, 2) + lead_shape(full) + (16, width_of(full) // 2), BF))
        for st in range(3):
            full = ORDERS[t][: 2 - st]
            scratch.append(pltpu.VMEM((2, 3 if st else 2) + lead_shape(full) + (16, width_of(full)), BF))
    out, app = pl.pallas_call(
        kernel,
        out_shape=(
            jax.ShapeDtypeStruct((2, 4, 3, 16, 1024), BF),
            jax.ShapeDtypeStruct((2, 2, 16, 128), BF),
        ),
        in_specs=[anyspace, vmem, vmem] + [anyspace] * 9 + [smem, smem, vmem],
        out_specs=(anyspace, vmem),
        scratch_shapes=scratch,
        compiler_params=pltpu.CompilerParams(
            collective_id=0, has_side_effects=True, vmem_limit_bytes=63 * 1024 * 1024
        ),
    )(
        embeds.reshape(2, 4, 3, 16, 1024),
        attn_gain,
        ffn_gain,
        query_weight.reshape(8, 2, 1024, 128),
        key_matrix.T,
        value_matrix.T,
        output_weight,
        gate_weight.T,
        up_weight.T,
        down_weight,
        rotated_key_cache.reshape(LOCAL, SLOTS, HEAD),
        stored_value_cache.reshape(LOCAL, SLOTS, HEAD),
        lengths,
        positions,
        freq,
    )
    return out.reshape(2, ROWS, 1024), app[:, :, :LOCAL].transpose(0, 2, 1, 3)


def solution(mesh):
    in_specs = (
        P(None, None, "col"),
        P("col"),
        P("col"),
        P(None, ("row", "col")),
        P(None, ("row", "col")),
        P(None, ("row", "col")),
        P(("row", "col"), None),
        P(None, ("row", "col")),
        P(None, ("row", "col")),
        P(("row", "col"), None),
        P("col", "row", None, None),
        P("col", "row", None, None),
        P("col"),
        P("col"),
    )
    out_specs = (P(None, None, "col"), P(None, "col", None, "row"))
    return jax.shard_map(on_device, mesh=mesh, in_specs=in_specs, out_specs=out_specs, check_vma=False)
```

```python
import functools

import jax
import jax.numpy as jnp
from jax import lax
from jax.experimental import pallas as pl
from jax.experimental.pallas import tpu as pltpu
from jax.sharding import PartitionSpec as P

WIDTH = 16384
HEAD = 128
STEPS = 2
SLOTS = 1024
EPS = 1e-05
THETA = 500000.0
ROWS = 192
LOCAL = 12
FFL = 104
BF = jnp.bfloat16
F32 = jnp.float32
MESH = pl.DeviceIdType.MESH
ORDERS = (("x", "y", "z"), ("y", "z", "x"), ("z", "x", "y"))
NT = (((1,), (1,)), ((), ()))
FAR_FIRST = (8, 9, 7, 10, 6, 11, 5, 12, 4, 13, 3, 14, 2, 15, 1)


def coords():
    row = lax.axis_index("row")
    col = lax.axis_index("col")
    return dict(x=(row // 4) * 2 + (col // 2) % 2, y=row % 4, z=col // 4, k=col % 2)


def device(c):
    return {"row": (c["x"] // 2) * 4 + c["y"], "col": c["z"] * 4 + (c["x"] % 2) * 2 + c["k"]}


def moved(c, d, s):
    e = dict(c)
    e[d] = (c[d] + s + 4) % 4
    return e


def remote(src, dst, ss, rs, target):
    return pltpu.make_async_remote_copy(
        src_ref=src, dst_ref=dst, send_sem=ss, recv_sem=rs, device_id=target, device_id_type=MESH
    )


def block(ref, t, c, full, d, q, sub, half=None):
    pos = dict(c)
    pos[d] = q
    z = slice(None) if "z" in full else pos["z"]
    y = slice(None) if "y" in full else pos["y"]
    xl = slice(None) if "x" in full else pos["x"] % 2
    xh = slice(None) if "x" in full else pos["x"] // 2
    columns = pl.ds(sub * 256, 256) if half is None else pl.ds(sub * 256 + half * 128, 128)
    return ref.at[z, xl, xh, y, t, :, columns]


def lead_shape(full):
    return ((4,) if "z" in full else ()) + ((2, 2) if "x" in full else ()) + ((4,) if "y" in full else ())


def for_parts(shape, body):
    if len(shape) < 2:
        body(())
    else:

        def step(n, carry):
            body((n,))
            return carry

        lax.fori_loop(0, shape[0], step, 0)


WAYS = ((0, 1), (1, -1))


def counted(ref, n):
    columns = pl.ds(0, 256)
    if n == 9:
        return ref.at[0, 0, 0, pl.ds(0, 3), :, :, columns]
    if n == 36:
        return ref.at[0, :, :, pl.ds(0, 3), :, :, columns]
    return ref.at[pl.ds(0, n // 48), :, :, :, :, :, columns]


def wait_for(ref, n, sem):
    part = counted(ref, n)
    pltpu.make_async_copy(part, part, sem).wait()


def drain(ref, ss, counts):
    for i, n in enumerate(counts):
        wait_for(ref, n, ss.at[i])


GATHERED = (9, 36, 144)
SCATTERED = (144, 36, 9)


def gather(g, c, ss, rs, sub):
    def send(src, d, s, ph, sem):
        remote(src, src, ss.at[ph], rs.at[sem], device(moved(c, d, s))).start()

    for ph in range(2):
        for o in (1, 3, 2):
            for t in range(3):
                d = ORDERS[t][ph]
                send(block(g, t, c, ORDERS[t][:ph], d, c[d], sub), d, o, ph, ph)
        yield
        wait_for(g, 9 * 4**ph, rs.at[ph])
    axes = [(t, ORDERS[t][2], ORDERS[t][:2]) for t in range(3)]
    for part in (0, 1):
        for t, d, full in axes:
            for i, s in WAYS:
                h = i if part == 0 else 1 - i
                send(block(g, t, c, full, d, c[d], sub, h), d, s, 2, 3 + 2 * t + i if part == 0 else 2)
    yield
    for t, d, full in axes:
        for i, s in WAYS:
            h = block(g, t, c, full, d, (c[d] - s + 4) % 4, sub, i)
            pltpu.make_async_copy(h, h, rs.at[3 + 2 * t + i]).wait()
            send(h, d, s, 2, 2)
    yield
    wait_for(g, 96, rs.at[2])


def scatter(p, fwd, land, c, ss, rs, sub):
    def send(src, dst, d, s, st, sem):
        remote(src, dst, ss.at[st], rs.at[sem], device(moved(c, d, s))).start()

    axes = [(t, ORDERS[t][2], ORDERS[t][:2]) for t in range(3)]

    def half(t, i, full, h):
        lead = (slice(None),) * len(lead_shape(full))
        return land[t][0].at[(i,) + lead + (slice(None), pl.ds(h * 128, 128))]

    for t, d, full in axes:
        for i, s in WAYS:
            send(block(p, t, c, full, d, (c[d] + 2) % 4, sub, i), fwd[t].at[i], d, s, 0, 3 + 2 * t + i)
    for t, d, full in axes:
        for i, s in WAYS:
            send(block(p, t, c, full, d, (c[d] + s + 4) % 4, sub, 1 - i), half(t, i, full, 1 - i), d, s, 0, 0)
    yield
    for t, d, full in axes:
        for i, s in WAYS:
            f = fwd[t].at[i]
            pltpu.make_async_copy(f, f, rs.at[3 + 2 * t + i]).wait()
            mine = block(p, t, c, full, d, (c[d] + s + 4) % 4, sub, i)

            def add(idx, mine=mine, t=t, i=i):
                a = mine[idx].astype(F32) + fwd[t][(i,) + idx].astype(F32)
                mine[idx] = a.astype(BF)

            for_parts(lead_shape(full), add)
            send(mine, half(t, i, full, i), d, s, 0, 0)
    yield
    wait_for(p, 96, rs.at[0])
    for t, d, full in axes:
        mine = block(p, t, c, full, d, c[d], sub)

        def total(idx, mine=mine, t=t):
            a = mine[idx].astype(F32) + (land[t][0][(0,) + idx].astype(F32) + land[t][0][(1,) + idx].astype(F32))
            mine[idx] = a.astype(BF)

        for_parts(lead_shape(full), total)
    for st in (1, 2):
        axes = [(t, ORDERS[t][2 - st], ORDERS[t][: 2 - st]) for t in range(3)]
        for o in (1, 3, 2):
            for t, d, full in axes:
                send(block(p, t, c, full, d, (c[d] + o) % 4, sub), land[t][st].at[o - 1], d, o, st, st)
        yield
        wait_for(p, 36 // 4 ** (st - 1), rs.at[st])
        for t, d, full in axes:
            mine = block(p, t, c, full, d, c[d], sub)
            a = mine[...].astype(F32)
            for o in range(3):
                a = a + land[t][st][o].astype(F32)
            mine[...] = a.astype(BF)


def in_turn(a, b):
    for _ in a:
        yield
        next(b)
        yield
    for _ in b:
        yield


def iota(shape, d):
    return lax.broadcasted_iota(jnp.int32, shape, d)


def onehot(cond):
    return jnp.where(cond, 1.0, 0.0).astype(BF)


def mm(a, b):
    return jnp.dot(a, b, preferred_element_type=F32)


def mm_nt(a, b):
    return lax.dot_general(a, b, NT, preferred_element_type=F32)


def kernel(*refs):
    names = (
        "emb_h", "attn_gain", "ffn_gain", "wq_h", "kh_h", "vh_h", "wo_h", "g_h", "u_h", "wd_h", "kc_h", "vc_h", "lens",
        "pos", "freq", "out", "app", "g", "p", "emb", "wq", "kv", "wo", "gate", "up", "wd", "kc", "vc", "ginv",
        "acc", "ssq", "qs", "qr", "kn", "vn", "qb", "sbuf", "pb", "ho", "hr", "xs", "xr", "res", "fin", "to_rows",
        "to_tokens", "by_row", "by_head", "spread", "place", "load_sem", "load_out", "pair_s", "pair_r", "ag_s",
        "ag_r", "rs_s", "rs_r", "a2a_s", "a2a_r", "gi_s", "gi_r", "x_s", "x_r", "f_s", "f_r",
    )
    n = dict(zip(names, refs[: len(names)]))
    rest = refs[len(names) :]
    r = type("Refs", (), n)
    c = coords()
    k = c["k"]
    col = lax.axis_index("col")
    row = lax.axis_index("row")
    xl, xh, y, z = c["x"] % 2, c["x"] // 2, c["y"], c["z"]
    mate = {"row": row, "col": col + 1 - 2 * k}
    far = dict(c)
    far["x"] = (c["x"] + 2) % 4

    def peer(o):
        return {"row": row, "col": (col + o) % 16}

    loads = {}

    def load(name, i, src, dst):
        cp = pltpu.make_async_copy(src, dst, r.load_sem.at[i])
        cp.start()
        loads[name] = cp

    load("emb", 0, r.emb_h, r.emb)

    bar = pltpu.get_barrier_semaphore()
    greet = [peer(o) for o in range(1, 16)]
    greet += [device(moved(c, "y", 1)), device(moved(c, "y", 2)), device(moved(c, "y", 3)), device(far)]
    other = dict(c)
    other["x"] = (c["x"] + 3 - 2 * (c["x"] % 2)) % 4
    greet.append(device(other))
    for target in greet:
        pl.semaphore_signal(bar, inc=1, device_id=target, device_id_type=MESH)
    pl.semaphore_wait(bar, len(greet))

    pair = {}

    def share(i, src_of, dst, blocks):
        for b in blocks:
            remote(src_of(1 - k, b), dst.at[(k,) + b], r.pair_s.at[i], r.pair_r.at[i], mate).start()
            pltpu.make_async_copy(src_of(k, b), dst.at[(k,) + b], r.load_sem.at[i]).start()

    def share_wait(i, dst):
        pltpu.make_async_copy(dst.at[k], dst.at[k], r.load_sem.at[i]).wait()
        whole = remote(dst.at[k], dst.at[1 - k], r.pair_s.at[i], r.pair_r.at[i], mate)
        whole.wait_recv()
        pair[i] = whole

    def lanes(ref):
        return lambda par, b: ref.at[:, pl.ds(pl.multiple_of((2 * b[0] + par) * 1024, 1024), 1024)]

    eight = [(b,) for b in range(8)]

    ga = r.attn_gain[...].astype(F32).reshape(1, 1024)
    gf = r.ffn_gain[...].astype(F32).reshape(1, 1024)
    r.ginv[z * 2 + xl] = jnp.where(iota((8, 1024), 0) == 0, 1.0 / (ga * ga), 1.0 / (gf * gf))

    def own(ref, t, sub):
        return block(ref, t, c, (), "z", z, sub)

    def cols(sub):
        return pl.ds(pl.multiple_of(xh * 512 + sub * 256, 256), 256)

    loads["emb"].wait()
    gain_a = jnp.where(xh == 0, ga[:, :512], ga[:, 512:])
    gain_f = jnp.where(xh == 0, gf[:, :512], gf[:, 512:])

    def emb_piece(s, t, sub):
        return r.emb[s, y, t, :, cols(sub)].astype(F32)

    def halves(ref, zz, xx):
        return jnp.concatenate([ref[zz, xx, h].reshape(ROWS, 512) for h in range(2)], axis=1)

    def put(ref, zz, xx, v):
        for h in range(2):
            ref[zz, xx, h] = v[:, h * 512 : (h + 1) * 512].astype(BF).reshape(4, 3, 16, 512)

    def startup():
        for o in range(1, 8):
            dst = r.ginv.at[z * 2 + xl]
            remote(dst, dst, r.gi_s.at[0], r.gi_r.at[0], peer(2 * o)).start()
        share(1, lambda par, b: r.wq_h.at[:, par], r.wq, [()])
        share(2, lanes(r.kh_h), r.kv.at[0], eight)
        share(9, lanes(r.vh_h), r.kv.at[1], eight)
        load("kc", 7, r.kc_h, r.kc)
        load("vc", 8, r.vc_h, r.vc)
        share(3, lanes(r.wo_h), r.wo, eight)
        share(4, lanes(r.g_h), r.gate, eight)
        share(5, lanes(r.u_h), r.up, eight)
        share(6, lanes(r.wd_h), r.wd, eight)
        a, b = iota((256, ROWS), 0), iota((256, ROWS), 1)
        r.to_rows[...] = onehot(((a & 15) < LOCAL) & (b == (a >> 4) * LOCAL + (a & 15)))
        a, b = iota((ROWS, 256), 0), iota((ROWS, 256), 1)
        r.to_tokens[...] = onehot(((b & 15) < LOCAL) & (a == (b >> 4) * LOCAL + (b & 15)))
        r.by_row[...] = onehot(((a >> 4) == (b & 15)) & ((a & 15) == (b >> 4)))
        a, b = iota((256, ROWS), 0), iota((256, ROWS), 1)
        r.by_head[...] = onehot(((b >> 4) == (a & 15)) & ((b & 15) == (a >> 4)))
        a, b = iota((ROWS, 16), 0), iota((ROWS, 16), 1)
        r.spread[...] = onehot((a >> 4) == b)
        a, b = iota((128, 256), 0), iota((128, 256), 1)
        for src in range(16):
            head_col = (a >> 4) * 8 + (a & 7) + (src // 2) * 16 + ((a >> 3) & 1) * 128
            r.place[src] = onehot((a < 32) & (b == head_col))

    first = {"w": True}

    def squares(s, g, zz, xx, which):
        v = halves(g, zz, xx)
        gi_row = r.ginv[zz * 2 + xx, pl.ds(which, 1), :]
        acc = jnp.zeros((ROWS, 128), F32)
        for j in range(8):
            w = v[:, j * 128 : (j + 1) * 128].astype(F32)
            acc = acc + w * w * gi_row[:, j * 128 : (j + 1) * 128]
        r.ssq[s] += acc

    def stream(s):
        sends = []
        g, p = r.g.at[s], r.p.at[s]
        fwd = [[rest[t * 4].at[s, sub] for t in range(3)] for sub in range(2)]
        land = [[[rest[t * 4 + 1 + st].at[s, sub] for st in range(3)] for t in range(3)] for sub in range(2)]

        def gathered(sub):
            return gather(g, c, r.ag_s.at[s, sub], r.ag_r.at[s, sub], sub)

        def scattered(sub):
            return scatter(p, fwd[sub], land[sub], c, r.rs_s.at[s, sub], r.rs_r.at[s, sub], sub)

        def through(sub):
            drain(g, r.ag_s.at[s, sub], GATHERED)
            yield from scattered(sub)
            for t in range(3):
                v = (emb_piece(s, t, sub) + own(p, t, sub)[...].astype(F32)).astype(BF)
                r.res[s, sub, t] = v
                own(g, t, sub)[...] = (v.astype(F32) * gain_f[:, sub * 256 : sub * 256 + 256]).astype(BF)
            yield from gathered(sub)

        for sub in range(2):
            for t in range(3):
                own(g, t, sub)[...] = (emb_piece(s, t, sub) * gain_a[:, sub * 256 : sub * 256 + 256]).astype(BF)
        for step, _ in enumerate(in_turn(gathered(0), gathered(1))):
            if s == 0 and step == STARTUP:
                startup()
            yield

        if first.pop("w", False):
            share_wait(1, r.wq)
            share_wait(2, r.kv.at[0])
            share_wait(9, r.kv.at[1])
            part = r.ginv.at[pl.ds(0, 7)]
            pltpu.make_async_copy(part, part, r.gi_r.at[0]).wait()
        r.acc[s] = jnp.zeros((3, ROWS, 128), F32)
        r.ssq[s] = jnp.zeros((ROWS, 128), F32)

        def qkv(i, carry):
            zz, xx = i // 2, i % 2
            v = halves(g, zz, xx)
            wq = jnp.concatenate([r.wq[0, i], r.wq[1, i]], axis=1)
            q = mm(v, wq)
            r.acc[s, 0] += q[:, :128]
            r.acc[s, 1] += q[:, 128:]
            wkv = [r.kv[j, core, i].astype(F32) for core in range(2) for j in range(2)]
            wkv = jnp.concatenate(wkv, axis=0).astype(BF)
            r.acc[s, 2, :, pl.ds(0, 32)] += mm_nt(v, wkv)
            squares(s, g, zz, xx, 0)
            return carry

        lax.fori_loop(0, 4, qkv, 0)
        yield
        lax.fori_loop(4, 8, qkv, 0)
        total = jnp.sum(r.ssq[s], axis=-1, keepdims=True)
        high = total.astype(BF).astype(F32)
        low = total - high
        lane = iota((ROWS, 128), 1)
        tail = jnp.where(lane == 32, high, jnp.where(lane == 33, low, r.acc[s, 2]))
        sums = jnp.concatenate([r.acc[s, 0], r.acc[s, 1], tail], axis=1).astype(BF)
        r.qs[s] = mm(r.to_rows[...], sums).astype(BF).reshape(16, 16, 384)
        for o in FAR_FIRST:
            remote(r.qs.at[s, (col + o) % 16], r.qr.at[s, col], r.a2a_s.at[s, 0], r.a2a_r.at[s, 0], peer(o)).start()
        r.qr[s, col] = r.qs[s, col]
        yield
        part = r.qr.at[s, pl.ds(0, 15)]
        pltpu.make_async_copy(part, part, r.a2a_r.at[s, 0]).wait()

        ends = r.qr[s, 0, :, pl.ds(256, 128)].astype(F32) + r.qr[s, 1, :, pl.ds(256, 128)].astype(F32)
        l16 = iota((16, 128), 1)
        square = jnp.sum(jnp.where((l16 == 32) | (l16 == 33), ends, 0.0), axis=-1, keepdims=True)
        scale = lax.rsqrt(square / WIDTH + EPS)
        angle = jnp.zeros((16, 128), jnp.int32)
        for j in range(LOCAL):
            angle = jnp.where(iota((16, 128), 0) == j, r.pos[j] + s, angle)
        angle = angle.astype(F32) * r.freq[...]
        cos, sin = jnp.cos(angle), jnp.sin(angle)
        sin = jnp.where(l16 < 64, -sin, sin)

        def rotate(v):
            return (v * cos + pltpu.roll(v, 64, 1) * sin).astype(BF)

        heads = []
        for h in range(8):
            both = r.qr[s, 2 * h, :, pl.ds(0, 256)].astype(F32) + r.qr[s, 2 * h + 1, :, pl.ds(0, 256)].astype(F32)
            both = both * scale
            heads += [rotate(both[:, :128]), rotate(both[:, 128:])]
        q_all = mm(r.by_row[...], jnp.concatenate(heads, axis=0)).astype(BF)
        r.qb[s] = q_all
        kv = mm(r.qr[s, 0, :, pl.ds(256, 128)], r.place[0])
        for src in range(1, 16):
            kv = kv + mm(r.qr[s, src, :, pl.ds(256, 128)], r.place[src])
        kv = kv * scale
        r.kn[s] = rotate(kv[:, :128])
        r.vn[s] = kv[:, 128:].astype(BF)
        r.app[s, 0] = r.kn[s]
        r.app[s, 1] = r.vn[s]

        if s == 0:
            loads["kc"].wait()
            loads["vc"].wait()
        factor = 1.0 / (HEAD**0.5)
        slot = iota((16, SLOTS), 1)
        qf = r.qb[s].astype(F32)
        fresh = []
        top = None
        for s2 in range(s + 1):
            sc = jnp.sum(qf * mm(r.spread[...], r.kn[s2]), axis=-1, keepdims=True) * factor
            fresh.append(sc)
            top = sc if top is None else jnp.maximum(top, sc)
        for j in range(LOCAL):
            sc = mm_nt(r.qb[s, pl.ds(j * 16, 16), :], r.kc[j]) * factor
            r.sbuf[pl.ds(j * 16, 16), :] = jnp.where(slot < r.lens[j], sc, -1e30)
        dens = []
        tops = []
        for j in range(LOCAL):
            sc = r.sbuf[pl.ds(j * 16, 16), :]
            m = jnp.maximum(jnp.max(sc, axis=-1, keepdims=True), top[j * 16 : j * 16 + 16])
            w = jnp.exp(sc - m)
            r.pb[pl.ds(j * 16, 16), :] = w.astype(BF)
            dens.append(jnp.sum(w, axis=-1, keepdims=True))
            tops.append(m)
        den = jnp.concatenate(dens, axis=0)
        m = jnp.concatenate(tops, axis=0)
        o = jnp.concatenate([mm(r.pb[pl.ds(j * 16, 16), :], r.vc[j]) for j in range(LOCAL)], axis=0)
        for s2 in range(s + 1):
            w = jnp.exp(fresh[s2] - m)
            den = den + w
            o = o + w.astype(BF).astype(F32) * mm(r.spread[...], r.vn[s2])
        o = (o / den).astype(BF)
        ho = mm(r.by_head[...], o).astype(BF).reshape(8, 2, 16, 128)
        for h in range(8):
            r.ho[s, h] = jnp.concatenate([ho[h, 0], ho[h, 1]], axis=1)
        for o_ in FAR_FIRST:
            remote(
                r.ho.at[s, ((col + o_) % 16) // 2], r.hr.at[s, col], r.a2a_s.at[s, 1], r.a2a_r.at[s, 1], peer(o_)
            ).start()
        r.hr[s, col] = r.ho[s, col // 2]
        yield
        if s == 0:
            share_wait(3, r.wo)
        part = r.hr.at[s, pl.ds(0, 15)]
        pltpu.make_async_copy(part, part, r.a2a_r.at[s, 1]).wait()

        attn = mm(r.to_tokens[...], r.hr[s].reshape(256, 256)).astype(BF)

        def project(i, carry):
            w = jnp.concatenate([r.wo[0, i], r.wo[1, i]], axis=0)
            put(p, i // 2, i % 2, mm(attn, w))
            return carry

        lax.fori_loop(0, 8, project, 0)
        yield from in_turn(through(0), through(1))

        if s == 0:
            share_wait(4, r.gate)
            share_wait(5, r.up)
        gap = jnp.zeros((128 - FFL, 1024), BF)
        r.xs[s] = jnp.zeros((4, ROWS, 128), F32)
        r.ssq[s] = jnp.zeros((ROWS, 128), F32)

        def slab(i, carry):
            zz, xx = i // 2, i % 2
            v = halves(g, zz, xx)
            for core in range(2):
                w = jnp.concatenate([r.gate[core, i], gap, r.up[core, i], gap], axis=0)
                v2 = mm_nt(v, w)
                r.xs[s, core] += v2[:, :128]
                r.xs[s, 2 + core] += v2[:, 128:]
            squares(s, g, zz, xx, 1)
            return carry

        lax.fori_loop(0, 4, slab, 0)
        yield
        lax.fori_loop(4, 8, slab, 0)
        total = jnp.sum(r.ssq[s], axis=-1, keepdims=True)
        r.xs[s, 0] = jnp.where(lane < FFL, r.xs[s, 0], total)
        cp = remote(r.xs.at[s], r.xr.at[s], r.x_s.at[s], r.x_r.at[s], mate)
        cp.start()
        yield
        if s == 0:
            share_wait(6, r.wd)
        cp.wait()
        first_sum = r.xs[s, 0] + r.xr[s, 0]
        square = jnp.sum(jnp.where(lane == FFL, first_sum, 0.0), axis=-1, keepdims=True)
        scale = lax.rsqrt(square / WIDTH + EPS)
        hidden = []
        for core in range(2):
            gate = (first_sum if core == 0 else r.xs[s, core] + r.xr[s, core]) * scale
            up = (r.xs[s, 2 + core] + r.xr[s, 2 + core]) * scale
            act = gate / (1.0 + jnp.exp(-gate)) * up
            hidden.append(jnp.where(lane < FFL, act, 0.0).astype(BF))
        hidden = jnp.concatenate(hidden, axis=1)

        def down(i, carry):
            v = mm(hidden, jnp.concatenate([r.wd[0, i], gap, r.wd[1, i], gap], axis=0))
            put(p, i // 2, i % 2, v)
            return carry

        for sub in range(2):
            drain(p, r.rs_s.at[s, sub], SCATTERED)
        lax.fori_loop(0, 8, down, 0)
        yield from in_turn(scattered(0), scattered(1))

        def fpiece(yy, hh):
            return r.fin.at[s, yy, :, :, pl.ds(pl.multiple_of(hh * 512, 512), 512)]

        for t in range(3):
            for sub in range(2):
                v = r.res[s, sub, t].astype(F32) + own(p, t, sub)[...].astype(F32)
                r.fin[s, y, t, :, cols(sub)] = v.astype(BF)
        mine = fpiece(y, xh)

        def fsend(piece, target, i):
            cp = remote(piece, piece, r.f_s.at[s, i], r.f_r.at[s, i], target)
            cp.start()
            sends.append(cp)

        def farrive(piece, i):
            remote(piece, piece, r.f_s.at[s, i], r.f_r.at[s, i], mate).wait_recv()

        theirs = fpiece(y, 1 - xh)
        fsend(mine, device(far), 0)
        for o_ in (2, 1, 3):
            fsend(mine, device(moved(c, "y", o_)), o_)
        yield
        farrive(theirs, 0)
        for o_ in (2, 1, 3):
            fsend(theirs, device(moved(c, "y", o_)), 3 + o_)
        yield
        for o_ in (1, 2, 3):
            farrive(fpiece((y + 4 - o_) % 4, xh), o_)
        for o_ in (1, 2, 3):
            farrive(fpiece((y + 4 - o_) % 4, 1 - xh), 3 + o_)
        cp = pltpu.make_async_copy(r.fin.at[s], r.out.at[s], r.load_out.at[s])
        cp.start()
        for e in sends:
            e.wait_send()
        for sub in range(2):
            drain(g, r.ag_s.at[s, sub], GATHERED)
            drain(p, r.rs_s.at[s, sub], SCATTERED)
        for i, ref in ((0, r.qr), (1, r.hr)):
            part = ref.at[s, pl.ds(0, 15)]
            pltpu.make_async_copy(part, part, r.a2a_s.at[s, i]).wait()
        cp.wait()

    live = [stream(s) for s in range(STEPS)]
    for s in "".join(SCHEDULE):
        next(live[int(s)], None)
    for it in live:
        for _ in it:
            pass
    part = r.ginv.at[pl.ds(0, 7)]
    pltpu.make_async_copy(part, part, r.gi_s.at[0]).wait()
    for i in pair:
        pair[i].wait_send()


STARTUP = 3
SCHEDULE = (
    "0101001000011001110110010001001100110011001101",
    "1001110101001100111010110011010101100110011100",
)


def finish(out_in, app_in, out, app):
    out[...] = out_in[...]
    for s in range(STEPS):
        both = [app_in[s, i].astype(F32)[:LOCAL].reshape(LOCAL, 1, HEAD) for i in range(2)]
        app[s] = jnp.concatenate(both, axis=1).astype(BF)


def rope_frequency(head_size):
    half_size = head_size // 2
    return THETA ** (-2.0 * jnp.arange(half_size, dtype=jnp.float32) / head_size)


def on_device(
    embeds,
    attn_gain,
    ffn_gain,
    query_weight,
    key_matrix,
    value_matrix,
    output_weight,
    gate_weight,
    up_weight,
    down_weight,
    rotated_key_cache,
    stored_value_cache,
    lengths,
    positions,
):
    freq = rope_frequency(HEAD)
    freq = jnp.concatenate([freq, freq]).reshape(1, HEAD)
    anyspace = pl.BlockSpec(memory_space=pl.ANY)
    vmem = pl.BlockSpec(memory_space=pltpu.VMEM)
    smem = pl.BlockSpec(memory_space=pltpu.SMEM)
    scratch = [
        pltpu.VMEM((2, 4, 2, 2, 4, 3, 16, 512), BF),
        pltpu.VMEM((2, 4, 2, 2, 4, 3, 16, 512), BF),
        pltpu.VMEM((2, 4, 3, 16, 1024), BF),
        pltpu.VMEM((2, 8, 1024, 128), BF),
        pltpu.VMEM((2, 2, 8, 8, 1024), BF),
        pltpu.VMEM((2, 8, 128, 1024), BF),
        pltpu.VMEM((2, 8, FFL, 1024), BF),
        pltpu.VMEM((2, 8, FFL, 1024), BF),
        pltpu.VMEM((2, 8, FFL, 1024), BF),
        pltpu.VMEM((LOCAL, SLOTS, HEAD), BF),
        pltpu.VMEM((LOCAL, SLOTS, HEAD), BF),
        pltpu.VMEM((8, 8, 1024), F32),
        pltpu.VMEM((2, 3, ROWS, 128), F32),
        pltpu.VMEM((2, ROWS, 128), F32),
        pltpu.VMEM((2, 16, 16, 384), BF),
        pltpu.VMEM((2, 16, 16, 384), BF),
        pltpu.VMEM((2, 16, 128), BF),
        pltpu.VMEM((2, 16, 128), BF),
        pltpu.VMEM((2, ROWS, 128), BF),
        pltpu.VMEM((ROWS, SLOTS), F32),
        pltpu.VMEM((ROWS, SLOTS), BF),
        pltpu.VMEM((2, 8, 16, 256), BF),
        pltpu.VMEM((2, 16, 16, 256), BF),
        pltpu.VMEM((2, 4, ROWS, 128), F32),
        pltpu.VMEM((2, 4, ROWS, 128), F32),
        pltpu.VMEM((2, 2, 3, 16, 256), BF),
        pltpu.VMEM((2, 4, 3, 16, 1024), BF),
        pltpu.VMEM((256, ROWS), BF),
        pltpu.VMEM((ROWS, 256), BF),
        pltpu.VMEM((ROWS, 256), BF),
        pltpu.VMEM((256, ROWS), BF),
        pltpu.VMEM((ROWS, 16), BF),
        pltpu.VMEM((16, 128, 256), BF),
        pltpu.SemaphoreType.DMA((10,)),
        pltpu.SemaphoreType.DMA((2,)),
        pltpu.SemaphoreType.DMA((10,)),
        pltpu.SemaphoreType.DMA((10,)),
        pltpu.SemaphoreType.DMA((2, 2, 3)),
        pltpu.SemaphoreType.DMA((2, 2, 9)),
        pltpu.SemaphoreType.DMA((2, 2, 3)),
        pltpu.SemaphoreType.DMA((2, 2, 9)),
        pltpu.SemaphoreType.DMA((2, 2)),
        pltpu.SemaphoreType.DMA((2, 2)),
        pltpu.SemaphoreType.DMA((1,)),
        pltpu.SemaphoreType.DMA((1,)),
        pltpu.SemaphoreType.DMA((2,)),
        pltpu.SemaphoreType.DMA((2,)),
        pltpu.SemaphoreType.DMA((2, 7)),
        pltpu.SemaphoreType.DMA((2, 7)),
    ]
    for t in range(3):
        full = ORDERS[t][:2]
        scratch.append(pltpu.VMEM((2, 2, 2) + lead_shape(full) + (16, 128), BF))
        for st in range(3):
            full = ORDERS[t][: 2 - st]
            scratch.append(pltpu.VMEM((2, 2, 3 if st else 2) + lead_shape(full) + (16, 256), BF))
    out, app = pl.pallas_call(
        kernel,
        out_shape=(
            jax.ShapeDtypeStruct((2, 4, 3, 16, 1024), BF),
            jax.ShapeDtypeStruct((2, 2, 16, 128), BF),
        ),
        in_specs=[anyspace, vmem, vmem] + [anyspace] * 9 + [smem, smem, vmem],
        out_specs=(anyspace, vmem),
        scratch_shapes=scratch,
        compiler_params=pltpu.CompilerParams(
            collective_id=0, has_side_effects=True, vmem_limit_bytes=63 * 1024 * 1024
        ),
    )(
        embeds.reshape(2, 4, 3, 16, 1024),
        attn_gain,
        ffn_gain,
        query_weight.reshape(8, 2, 1024, 128),
        key_matrix.T,
        value_matrix.T,
        output_weight,
        gate_weight.T,
        up_weight.T,
        down_weight,
        rotated_key_cache.reshape(LOCAL, SLOTS, HEAD),
        stored_value_cache.reshape(LOCAL, SLOTS, HEAD),
        lengths,
        positions,
        freq,
    )
    return pl.pallas_call(
        finish,
        out_shape=(
            jax.ShapeDtypeStruct((2, ROWS, 1024), BF),
            jax.ShapeDtypeStruct((2, LOCAL, 2, HEAD), BF),
        ),
        in_specs=[vmem, vmem],
        out_specs=(vmem, vmem),
    )(out.reshape(2, ROWS, 1024), app)


def solution(mesh):
    in_specs = (
        P(None, None, "col"),
        P("col"),
        P("col"),
        P(None, ("row", "col")),
        P(None, ("row", "col")),
        P(None, ("row", "col")),
        P(("row", "col"), None),
        P(None, ("row", "col")),
        P(None, ("row", "col")),
        P(("row", "col"), None),
        P("col", "row", None, None),
        P("col", "row", None, None),
        P("col"),
        P("col"),
    )
    out_specs = (P(None, None, "col"), P(None, "col", None, "row"))
    return jax.shard_map(on_device, mesh=mesh, in_specs=in_specs, out_specs=out_specs, check_vma=False)
```

```python
import functools

import jax
import jax.numpy as jnp
from jax import lax
from jax.experimental import pallas as pl
from jax.experimental.pallas import tpu as pltpu
from jax.sharding import PartitionSpec as P

WIDTH = 16384
HEAD = 128
STEPS = 2
SLOTS = 1024
EPS = 1e-05
THETA = 500000.0
ROWS = 192
LOCAL = 12
FFL = 104
BF = jnp.bfloat16
F32 = jnp.float32
MESH = pl.DeviceIdType.MESH
ORDERS = (("x", "y", "z"), ("y", "z", "x"), ("z", "x", "y"))
NT = (((1,), (1,)), ((), ()))
FAR_FIRST = (8, 9, 7, 10, 6, 11, 5, 12, 4, 13, 3, 14, 2, 15, 1)


def coords():
    row = lax.axis_index("row")
    col = lax.axis_index("col")
    return dict(x=(row // 4) * 2 + (col // 2) % 2, y=row % 4, z=col // 4, k=col % 2)


def device(c):
    return {"row": (c["x"] // 2) * 4 + c["y"], "col": c["z"] * 4 + (c["x"] % 2) * 2 + c["k"]}


def moved(c, d, s):
    e = dict(c)
    e[d] = (c[d] + s + 4) % 4
    return e


def remote(src, dst, ss, rs, target):
    return pltpu.make_async_remote_copy(
        src_ref=src, dst_ref=dst, send_sem=ss, recv_sem=rs, device_id=target, device_id_type=MESH
    )


def block(ref, t, c, full, d, q, sub, half=None):
    pos = dict(c)
    pos[d] = q
    z = slice(None) if "z" in full else pos["z"]
    y = slice(None) if "y" in full else pos["y"]
    xl = slice(None) if "x" in full else pos["x"] % 2
    xh = slice(None) if "x" in full else pos["x"] // 2
    columns = pl.ds(sub * 256, 256) if half is None else pl.ds(sub * 256 + half * 128, 128)
    return ref.at[z, xl, xh, y, t, :, columns]


def lead_shape(full):
    return ((4,) if "z" in full else ()) + ((2, 2) if "x" in full else ()) + ((4,) if "y" in full else ())


def for_parts(shape, body):
    if len(shape) < 2:
        body(())
    else:

        def step(n, carry):
            body((n,))
            return carry

        lax.fori_loop(0, shape[0], step, 0)


WAYS = ((0, 1), (1, -1))


def counted(ref, n):
    columns = pl.ds(0, 256)
    if n == 9:
        return ref.at[0, 0, 0, pl.ds(0, 3), :, :, columns]
    if n == 36:
        return ref.at[0, :, :, pl.ds(0, 3), :, :, columns]
    return ref.at[pl.ds(0, n // 48), :, :, :, :, :, columns]


def wait_for(ref, n, sem):
    part = counted(ref, n)
    pltpu.make_async_copy(part, part, sem).wait()


def drain(ref, ss, counts):
    for i, n in enumerate(counts):
        wait_for(ref, n, ss.at[i])


GATHERED = (9, 36, 144)
SCATTERED = (144, 36, 9)


def gather(g, c, ss, rs, sub):
    def send(src, d, s, ph, sem):
        remote(src, src, ss.at[ph], rs.at[sem], device(moved(c, d, s))).start()

    for ph in range(2):
        for o in (1, 3, 2):
            for t in range(3):
                d = ORDERS[t][ph]
                send(block(g, t, c, ORDERS[t][:ph], d, c[d], sub), d, o, ph, ph)
        yield
        wait_for(g, 9 * 4**ph, rs.at[ph])
    axes = [(t, ORDERS[t][2], ORDERS[t][:2]) for t in range(3)]
    for part in (0, 1):
        for t, d, full in axes:
            for i, s in WAYS:
                h = i if part == 0 else 1 - i
                send(block(g, t, c, full, d, c[d], sub, h), d, s, 2, 3 + 2 * t + i if part == 0 else 2)
    yield
    for t, d, full in axes:
        for i, s in WAYS:
            h = block(g, t, c, full, d, (c[d] - s + 4) % 4, sub, i)
            pltpu.make_async_copy(h, h, rs.at[3 + 2 * t + i]).wait()
            send(h, d, s, 2, 2)
    yield
    wait_for(g, 96, rs.at[2])


def scatter(p, fwd, land, c, ss, rs, sub):
    def send(src, dst, d, s, st, sem):
        remote(src, dst, ss.at[st], rs.at[sem], device(moved(c, d, s))).start()

    axes = [(t, ORDERS[t][2], ORDERS[t][:2]) for t in range(3)]

    def half(t, i, full, h):
        lead = (slice(None),) * len(lead_shape(full))
        return land[t][0].at[(i,) + lead + (slice(None), pl.ds(h * 128, 128))]

    for t, d, full in axes:
        for i, s in WAYS:
            send(block(p, t, c, full, d, (c[d] + 2) % 4, sub, i), fwd[t].at[i], d, s, 0, 3 + 2 * t + i)
    for t, d, full in axes:
        for i, s in WAYS:
            send(block(p, t, c, full, d, (c[d] + s + 4) % 4, sub, 1 - i), half(t, i, full, 1 - i), d, s, 0, 0)
    yield
    for t, d, full in axes:
        for i, s in WAYS:
            f = fwd[t].at[i]
            pltpu.make_async_copy(f, f, rs.at[3 + 2 * t + i]).wait()
            mine = block(p, t, c, full, d, (c[d] + s + 4) % 4, sub, i)

            def add(idx, mine=mine, t=t, i=i):
                a = mine[idx].astype(F32) + fwd[t][(i,) + idx].astype(F32)
                mine[idx] = a.astype(BF)

            for_parts(lead_shape(full), add)
            send(mine, half(t, i, full, i), d, s, 0, 0)
    yield
    wait_for(p, 96, rs.at[0])
    for t, d, full in axes:
        mine = block(p, t, c, full, d, c[d], sub)

        def total(idx, mine=mine, t=t):
            a = mine[idx].astype(F32) + (land[t][0][(0,) + idx].astype(F32) + land[t][0][(1,) + idx].astype(F32))
            mine[idx] = a.astype(BF)

        for_parts(lead_shape(full), total)
    for st in (1, 2):
        axes = [(t, ORDERS[t][2 - st], ORDERS[t][: 2 - st]) for t in range(3)]
        for o in (1, 3, 2):
            for t, d, full in axes:
                send(block(p, t, c, full, d, (c[d] + o) % 4, sub), land[t][st].at[o - 1], d, o, st, st)
        yield
        wait_for(p, 36 // 4 ** (st - 1), rs.at[st])
        for t, d, full in axes:
            mine = block(p, t, c, full, d, c[d], sub)
            a = mine[...].astype(F32)
            for o in range(3):
                a = a + land[t][st][o].astype(F32)
            mine[...] = a.astype(BF)


def in_turn(a, b):
    for _ in a:
        yield
        next(b)
        yield
    for _ in b:
        yield


def iota(shape, d):
    return lax.broadcasted_iota(jnp.int32, shape, d)


def onehot(cond):
    return jnp.where(cond, 1.0, 0.0).astype(BF)


def mm(a, b):
    return jnp.dot(a, b, preferred_element_type=F32)


def mm_nt(a, b):
    return lax.dot_general(a, b, NT, preferred_element_type=F32)


def kernel(*refs):
    names = (
        "emb_h", "attn_gain", "ffn_gain", "wq_h", "kh_h", "vh_h", "wo_h", "g_h", "u_h", "wd_h", "kc_h", "vc_h", "lens",
        "pos", "freq", "out", "app", "g", "p", "emb", "wq", "kv", "wo", "gate", "up", "wd", "kc", "vc", "ginv",
        "acc", "ssq", "qs", "qr", "kn", "vn", "qb", "sbuf", "pb", "ho", "hr", "xs", "xr", "res", "fin", "to_rows",
        "to_tokens", "by_row", "by_head", "spread", "place", "load_sem", "load_out", "pair_s", "pair_r", "ag_s",
        "ag_r", "rs_s", "rs_r", "a2a_s", "a2a_r", "gi_s", "gi_r", "x_s", "x_r", "f_s", "f_r",
    )
    n = dict(zip(names, refs[: len(names)]))
    rest = refs[len(names) :]
    r = type("Refs", (), n)
    c = coords()
    k = c["k"]
    col = lax.axis_index("col")
    row = lax.axis_index("row")
    xl, xh, y, z = c["x"] % 2, c["x"] // 2, c["y"], c["z"]
    mate = {"row": row, "col": col + 1 - 2 * k}
    far = dict(c)
    far["x"] = (c["x"] + 2) % 4

    def peer(o):
        return {"row": row, "col": (col + o) % 16}

    loads = {}

    def load(name, i, src, dst):
        cp = pltpu.make_async_copy(src, dst, r.load_sem.at[i])
        cp.start()
        loads[name] = cp

    load("emb", 0, r.emb_h, r.emb)

    bar = pltpu.get_barrier_semaphore()
    greet = [peer(o) for o in range(1, 16)]
    greet += [device(moved(c, "y", 1)), device(moved(c, "y", 2)), device(moved(c, "y", 3)), device(far)]
    other = dict(c)
    other["x"] = (c["x"] + 3 - 2 * (c["x"] % 2)) % 4
    greet.append(device(other))
    for target in greet:
        pl.semaphore_signal(bar, inc=1, device_id=target, device_id_type=MESH)
    pl.semaphore_wait(bar, len(greet))

    pair = {}

    def share(i, src_of, dst, blocks):
        for b in blocks:
            remote(src_of(1 - k, b), dst.at[(k,) + b], r.pair_s.at[i], r.pair_r.at[i], mate).start()
            pltpu.make_async_copy(src_of(k, b), dst.at[(k,) + b], r.load_sem.at[i]).start()

    def share_wait(i, dst):
        pltpu.make_async_copy(dst.at[k], dst.at[k], r.load_sem.at[i]).wait()
        whole = remote(dst.at[k], dst.at[1 - k], r.pair_s.at[i], r.pair_r.at[i], mate)
        whole.wait_recv()
        pair[i] = whole

    def lanes(ref):
        return lambda par, b: ref.at[:, pl.ds(pl.multiple_of((2 * b[0] + par) * 1024, 1024), 1024)]

    eight = [(b,) for b in range(8)]

    ga = r.attn_gain[...].astype(F32).reshape(1, 1024)
    gf = r.ffn_gain[...].astype(F32).reshape(1, 1024)
    r.ginv[z * 2 + xl] = jnp.where(iota((8, 1024), 0) == 0, 1.0 / (ga * ga), 1.0 / (gf * gf))

    def own(ref, t, sub):
        return block(ref, t, c, (), "z", z, sub)

    def cols(sub):
        return pl.ds(pl.multiple_of(xh * 512 + sub * 256, 256), 256)

    loads["emb"].wait()
    gain_a = jnp.where(xh == 0, ga[:, :512], ga[:, 512:])
    gain_f = jnp.where(xh == 0, gf[:, :512], gf[:, 512:])

    def emb_piece(s, t, sub):
        return r.emb[s, y, t, :, cols(sub)].astype(F32)

    def halves(ref, zz, xx):
        return jnp.concatenate([ref[zz, xx, h].reshape(ROWS, 512) for h in range(2)], axis=1)

    def put(ref, zz, xx, v):
        for h in range(2):
            ref[zz, xx, h] = v[:, h * 512 : (h + 1) * 512].astype(BF).reshape(4, 3, 16, 512)

    def startup():
        for o in range(1, 8):
            dst = r.ginv.at[z * 2 + xl]
            remote(dst, dst, r.gi_s.at[0], r.gi_r.at[0], peer(2 * o)).start()
        share(1, lambda par, b: r.wq_h.at[:, par], r.wq, [()])
        share(2, lanes(r.kh_h), r.kv.at[0], eight)
        share(9, lanes(r.vh_h), r.kv.at[1], eight)
        load("kc", 7, r.kc_h, r.kc)
        load("vc", 8, r.vc_h, r.vc)
        share(3, lanes(r.wo_h), r.wo, eight)
        share(4, lanes(r.g_h), r.gate, eight)
        share(5, lanes(r.u_h), r.up, eight)
        share(6, lanes(r.wd_h), r.wd, eight)
        a, b = iota((256, ROWS), 0), iota((256, ROWS), 1)
        r.to_rows[...] = onehot(((a & 15) < LOCAL) & (b == (a >> 4) * LOCAL + (a & 15)))
        a, b = iota((ROWS, 256), 0), iota((ROWS, 256), 1)
        r.to_tokens[...] = onehot(((b & 15) < LOCAL) & (a == (b >> 4) * LOCAL + (b & 15)))
        r.by_row[...] = onehot(((a >> 4) == (b & 15)) & ((a & 15) == (b >> 4)))
        a, b = iota((256, ROWS), 0), iota((256, ROWS), 1)
        r.by_head[...] = onehot(((b >> 4) == (a & 15)) & ((b & 15) == (a >> 4)))
        a, b = iota((ROWS, 16), 0), iota((ROWS, 16), 1)
        r.spread[...] = onehot((a >> 4) == b)
        a, b = iota((128, 256), 0), iota((128, 256), 1)
        for src in range(16):
            head_col = (a >> 4) * 8 + (a & 7) + (src // 2) * 16 + ((a >> 3) & 1) * 128
            r.place[src] = onehot((a < 32) & (b == head_col))

    first = {"w": True}

    def squares(s, g, zz, xx, which):
        v = halves(g, zz, xx)
        gi_row = r.ginv[zz * 2 + xx, pl.ds(which, 1), :]
        acc = jnp.zeros((ROWS, 128), F32)
        for j in range(8):
            w = v[:, j * 128 : (j + 1) * 128].astype(F32)
            acc = acc + w * w * gi_row[:, j * 128 : (j + 1) * 128]
        r.ssq[s] += acc

    def stream(s):
        sends = []
        g, p = r.g.at[s], r.p.at[s]
        fwd = [[rest[t * 4].at[s, sub] for t in range(3)] for sub in range(2)]
        land = [[[rest[t * 4 + 1 + st].at[s, sub] for st in range(3)] for t in range(3)] for sub in range(2)]

        def gathered(sub):
            return gather(g, c, r.ag_s.at[s, sub], r.ag_r.at[s, sub], sub)

        def scattered(sub):
            return scatter(p, fwd[sub], land[sub], c, r.rs_s.at[s, sub], r.rs_r.at[s, sub], sub)

        def through(sub):
            drain(g, r.ag_s.at[s, sub], GATHERED)
            yield from scattered(sub)
            for t in range(3):
                v = (emb_piece(s, t, sub) + own(p, t, sub)[...].astype(F32)).astype(BF)
                r.res[s, sub, t] = v
                own(g, t, sub)[...] = (v.astype(F32) * gain_f[:, sub * 256 : sub * 256 + 256]).astype(BF)
            yield from gathered(sub)

        for sub in range(2):
            for t in range(3):
                own(g, t, sub)[...] = (emb_piece(s, t, sub) * gain_a[:, sub * 256 : sub * 256 + 256]).astype(BF)
        for step, _ in enumerate(in_turn(gathered(0), gathered(1))):
            if s == 0 and step == STARTUP:
                startup()
            yield

        if first.pop("w", False):
            share_wait(1, r.wq)
            share_wait(2, r.kv.at[0])
            share_wait(9, r.kv.at[1])
            part = r.ginv.at[pl.ds(0, 7)]
            pltpu.make_async_copy(part, part, r.gi_r.at[0]).wait()
        r.acc[s] = jnp.zeros((3, ROWS, 128), F32)
        r.ssq[s] = jnp.zeros((ROWS, 128), F32)

        def qkv(i, carry):
            zz, xx = i // 2, i % 2
            v = halves(g, zz, xx)
            wq = jnp.concatenate([r.wq[0, i], r.wq[1, i]], axis=1)
            q = mm(v, wq)
            r.acc[s, 0] += q[:, :128]
            r.acc[s, 1] += q[:, 128:]
            wkv = [r.kv[j, core, i].astype(F32) for core in range(2) for j in range(2)]
            wkv = jnp.concatenate(wkv, axis=0).astype(BF)
            r.acc[s, 2, :, pl.ds(0, 32)] += mm_nt(v, wkv)
            squares(s, g, zz, xx, 0)
            return carry

        lax.fori_loop(0, 4, qkv, 0)
        yield
        lax.fori_loop(4, 8, qkv, 0)
        total = jnp.sum(r.ssq[s], axis=-1, keepdims=True)
        high = total.astype(BF).astype(F32)
        low = total - high
        lane = iota((ROWS, 128), 1)
        tail = jnp.where(lane == 32, high, jnp.where(lane == 33, low, r.acc[s, 2]))
        sums = jnp.concatenate([r.acc[s, 0], r.acc[s, 1], tail], axis=1).astype(BF)
        r.qs[s] = mm(r.to_rows[...], sums).astype(BF).reshape(16, 16, 384)
        for o in FAR_FIRST:
            remote(r.qs.at[s, (col + o) % 16], r.qr.at[s, col], r.a2a_s.at[s, 0], r.a2a_r.at[s, 0], peer(o)).start()
        r.qr[s, col] = r.qs[s, col]
        yield
        part = r.qr.at[s, pl.ds(0, 15)]
        pltpu.make_async_copy(part, part, r.a2a_r.at[s, 0]).wait()

        ends = r.qr[s, 0, :, pl.ds(256, 128)].astype(F32) + r.qr[s, 1, :, pl.ds(256, 128)].astype(F32)
        l16 = iota((16, 128), 1)
        square = jnp.sum(jnp.where((l16 == 32) | (l16 == 33), ends, 0.0), axis=-1, keepdims=True)
        scale = lax.rsqrt(square / WIDTH + EPS)
        angle = jnp.zeros((16, 128), jnp.int32)
        for j in range(LOCAL):
            angle = jnp.where(iota((16, 128), 0) == j, r.pos[j] + s, angle)
        angle = angle.astype(F32) * r.freq[...]
        cos, sin = jnp.cos(angle), jnp.sin(angle)
        sin = jnp.where(l16 < 64, -sin, sin)

        def rotate(v):
            return (v * cos + pltpu.roll(v, 64, 1) * sin).astype(BF)

        heads = []
        for h in range(8):
            both = r.qr[s, 2 * h, :, pl.ds(0, 256)].astype(F32) + r.qr[s, 2 * h + 1, :, pl.ds(0, 256)].astype(F32)
            both = both * scale
            heads += [rotate(both[:, :128]), rotate(both[:, 128:])]
        q_all = mm(r.by_row[...], jnp.concatenate(heads, axis=0)).astype(BF)
        r.qb[s] = q_all
        kv = mm(r.qr[s, 0, :, pl.ds(256, 128)], r.place[0])
        for src in range(1, 16):
            kv = kv + mm(r.qr[s, src, :, pl.ds(256, 128)], r.place[src])
        kv = kv * scale
        r.kn[s] = rotate(kv[:, :128])
        r.vn[s] = kv[:, 128:].astype(BF)
        r.app[s, 0] = r.kn[s]
        r.app[s, 1] = r.vn[s]

        if s == 0:
            loads["kc"].wait()
            loads["vc"].wait()
        factor = 1.0 / (HEAD**0.5)
        slot = iota((16, SLOTS), 1)
        qf = r.qb[s].astype(F32)
        fresh = []
        top = None
        for s2 in range(s + 1):
            sc = jnp.sum(qf * mm(r.spread[...], r.kn[s2]), axis=-1, keepdims=True) * factor
            fresh.append(sc)
            top = sc if top is None else jnp.maximum(top, sc)
        for j in range(LOCAL):
            sc = mm_nt(r.qb[s, pl.ds(j * 16, 16), :], r.kc[j]) * factor
            r.sbuf[pl.ds(j * 16, 16), :] = jnp.where(slot < r.lens[j], sc, -1e30)
        dens = []
        tops = []
        for j in range(LOCAL):
            sc = r.sbuf[pl.ds(j * 16, 16), :]
            m = jnp.maximum(jnp.max(sc, axis=-1, keepdims=True), top[j * 16 : j * 16 + 16])
            w = jnp.exp(sc - m)
            r.pb[pl.ds(j * 16, 16), :] = w.astype(BF)
            dens.append(jnp.sum(w, axis=-1, keepdims=True))
            tops.append(m)
        den = jnp.concatenate(dens, axis=0)
        m = jnp.concatenate(tops, axis=0)
        o = jnp.concatenate([mm(r.pb[pl.ds(j * 16, 16), :], r.vc[j]) for j in range(LOCAL)], axis=0)
        for s2 in range(s + 1):
            w = jnp.exp(fresh[s2] - m)
            den = den + w
            o = o + w.astype(BF).astype(F32) * mm(r.spread[...], r.vn[s2])
        o = (o / den).astype(BF)
        ho = mm(r.by_head[...], o).astype(BF).reshape(8, 2, 16, 128)
        for h in range(8):
            r.ho[s, h] = jnp.concatenate([ho[h, 0], ho[h, 1]], axis=1)
        for o_ in FAR_FIRST:
            remote(
                r.ho.at[s, ((col + o_) % 16) // 2], r.hr.at[s, col], r.a2a_s.at[s, 1], r.a2a_r.at[s, 1], peer(o_)
            ).start()
        r.hr[s, col] = r.ho[s, col // 2]
        yield
        if s == 0:
            share_wait(3, r.wo)
        part = r.hr.at[s, pl.ds(0, 15)]
        pltpu.make_async_copy(part, part, r.a2a_r.at[s, 1]).wait()

        attn = mm(r.to_tokens[...], r.hr[s].reshape(256, 256)).astype(BF)

        def project(i, carry):
            w = jnp.concatenate([r.wo[0, i], r.wo[1, i]], axis=0)
            put(p, i // 2, i % 2, mm(attn, w))
            return carry

        lax.fori_loop(0, 8, project, 0)
        yield from in_turn(through(0), through(1))

        if s == 0:
            share_wait(4, r.gate)
            share_wait(5, r.up)
        gap = jnp.zeros((128 - FFL, 1024), BF)
        r.xs[s] = jnp.zeros((4, ROWS, 128), F32)
        r.ssq[s] = jnp.zeros((ROWS, 128), F32)

        def slab(i, carry):
            zz, xx = i // 2, i % 2
            v = halves(g, zz, xx)
            for core in range(2):
                w = jnp.concatenate([r.gate[core, i], gap, r.up[core, i], gap], axis=0)
                v2 = mm_nt(v, w)
                r.xs[s, core] += v2[:, :128]
                r.xs[s, 2 + core] += v2[:, 128:]
            squares(s, g, zz, xx, 1)
            return carry

        lax.fori_loop(0, 4, slab, 0)
        yield
        lax.fori_loop(4, 8, slab, 0)
        total = jnp.sum(r.ssq[s], axis=-1, keepdims=True)
        r.xs[s, 0] = jnp.where(lane < FFL, r.xs[s, 0], total)
        cp = remote(r.xs.at[s], r.xr.at[s], r.x_s.at[s], r.x_r.at[s], mate)
        cp.start()
        yield
        if s == 0:
            share_wait(6, r.wd)
        cp.wait()
        first_sum = r.xs[s, 0] + r.xr[s, 0]
        square = jnp.sum(jnp.where(lane == FFL, first_sum, 0.0), axis=-1, keepdims=True)
        scale = lax.rsqrt(square / WIDTH + EPS)
        hidden = []
        for core in range(2):
            gate = (first_sum if core == 0 else r.xs[s, core] + r.xr[s, core]) * scale
            up = (r.xs[s, 2 + core] + r.xr[s, 2 + core]) * scale
            act = gate / (1.0 + jnp.exp(-gate)) * up
            hidden.append(jnp.where(lane < FFL, act, 0.0).astype(BF))
        hidden = jnp.concatenate(hidden, axis=1)

        def down(i, carry):
            v = mm(hidden, jnp.concatenate([r.wd[0, i], gap, r.wd[1, i], gap], axis=0))
            put(p, i // 2, i % 2, v)
            return carry

        for sub in range(2):
            drain(p, r.rs_s.at[s, sub], SCATTERED)
        lax.fori_loop(0, 8, down, 0)
        yield from in_turn(scattered(0), scattered(1))

        def fpiece(yy, hh):
            return r.fin.at[s, yy, :, :, pl.ds(pl.multiple_of(hh * 512, 512), 512)]

        for t in range(3):
            for sub in range(2):
                v = r.res[s, sub, t].astype(F32) + own(p, t, sub)[...].astype(F32)
                r.fin[s, y, t, :, cols(sub)] = v.astype(BF)
        mine = fpiece(y, xh)

        def fsend(piece, target, i):
            cp = remote(piece, piece, r.f_s.at[s, i], r.f_r.at[s, i], target)
            cp.start()
            sends.append(cp)

        def farrive(piece, i):
            remote(piece, piece, r.f_s.at[s, i], r.f_r.at[s, i], mate).wait_recv()

        theirs = fpiece(y, 1 - xh)
        fsend(mine, device(far), 0)
        for o_ in (2, 1, 3):
            fsend(mine, device(moved(c, "y", o_)), o_)
        yield
        farrive(theirs, 0)
        for o_ in (2, 1, 3):
            fsend(theirs, device(moved(c, "y", o_)), 3 + o_)
        yield
        for o_ in (1, 2, 3):
            farrive(fpiece((y + 4 - o_) % 4, xh), o_)
        for o_ in (1, 2, 3):
            farrive(fpiece((y + 4 - o_) % 4, 1 - xh), 3 + o_)
        cp = pltpu.make_async_copy(r.fin.at[s], r.out.at[s], r.load_out.at[s])
        cp.start()
        for e in sends:
            e.wait_send()
        for sub in range(2):
            drain(g, r.ag_s.at[s, sub], GATHERED)
            drain(p, r.rs_s.at[s, sub], SCATTERED)
        for i, ref in ((0, r.qr), (1, r.hr)):
            part = ref.at[s, pl.ds(0, 15)]
            pltpu.make_async_copy(part, part, r.a2a_s.at[s, i]).wait()
        cp.wait()

    live = [stream(s) for s in range(STEPS)]
    for s in "".join(SCHEDULE):
        next(live[int(s)], None)
    for it in live:
        for _ in it:
            pass
    part = r.ginv.at[pl.ds(0, 7)]
    pltpu.make_async_copy(part, part, r.gi_s.at[0]).wait()
    for i in pair:
        pair[i].wait_send()


STARTUP = 1
SCHEDULE = (
    "0101001000011001110110010001001100110011001101",
    "1001110101001100111010110011010101100110011100",
)


def finish(out_in, app_in, out, app):
    out[...] = out_in[...]
    for s in range(STEPS):
        both = [app_in[s, i].astype(F32)[:LOCAL].reshape(LOCAL, 1, HEAD) for i in range(2)]
        app[s] = jnp.concatenate(both, axis=1).astype(BF)


def rope_frequency(head_size):
    half_size = head_size // 2
    return THETA ** (-2.0 * jnp.arange(half_size, dtype=jnp.float32) / head_size)


def on_device(
    embeds,
    attn_gain,
    ffn_gain,
    query_weight,
    key_matrix,
    value_matrix,
    output_weight,
    gate_weight,
    up_weight,
    down_weight,
    rotated_key_cache,
    stored_value_cache,
    lengths,
    positions,
):
    freq = rope_frequency(HEAD)
    freq = jnp.concatenate([freq, freq]).reshape(1, HEAD)
    anyspace = pl.BlockSpec(memory_space=pl.ANY)
    vmem = pl.BlockSpec(memory_space=pltpu.VMEM)
    smem = pl.BlockSpec(memory_space=pltpu.SMEM)
    scratch = [
        pltpu.VMEM((2, 4, 2, 2, 4, 3, 16, 512), BF),
        pltpu.VMEM((2, 4, 2, 2, 4, 3, 16, 512), BF),
        pltpu.VMEM((2, 4, 3, 16, 1024), BF),
        pltpu.VMEM((2, 8, 1024, 128), BF),
        pltpu.VMEM((2, 2, 8, 8, 1024), BF),
        pltpu.VMEM((2, 8, 128, 1024), BF),
        pltpu.VMEM((2, 8, FFL, 1024), BF),
        pltpu.VMEM((2, 8, FFL, 1024), BF),
        pltpu.VMEM((2, 8, FFL, 1024), BF),
        pltpu.VMEM((LOCAL, SLOTS, HEAD), BF),
        pltpu.VMEM((LOCAL, SLOTS, HEAD), BF),
        pltpu.VMEM((8, 8, 1024), F32),
        pltpu.VMEM((2, 3, ROWS, 128), F32),
        pltpu.VMEM((2, ROWS, 128), F32),
        pltpu.VMEM((2, 16, 16, 384), BF),
        pltpu.VMEM((2, 16, 16, 384), BF),
        pltpu.VMEM((2, 16, 128), BF),
        pltpu.VMEM((2, 16, 128), BF),
        pltpu.VMEM((2, ROWS, 128), BF),
        pltpu.VMEM((ROWS, SLOTS), F32),
        pltpu.VMEM((ROWS, SLOTS), BF),
        pltpu.VMEM((2, 8, 16, 256), BF),
        pltpu.VMEM((2, 16, 16, 256), BF),
        pltpu.VMEM((2, 4, ROWS, 128), F32),
        pltpu.VMEM((2, 4, ROWS, 128), F32),
        pltpu.VMEM((2, 2, 3, 16, 256), BF),
        pltpu.VMEM((2, 4, 3, 16, 1024), BF),
        pltpu.VMEM((256, ROWS), BF),
        pltpu.VMEM((ROWS, 256), BF),
        pltpu.VMEM((ROWS, 256), BF),
        pltpu.VMEM((256, ROWS), BF),
        pltpu.VMEM((ROWS, 16), BF),
        pltpu.VMEM((16, 128, 256), BF),
        pltpu.SemaphoreType.DMA((10,)),
        pltpu.SemaphoreType.DMA((2,)),
        pltpu.SemaphoreType.DMA((10,)),
        pltpu.SemaphoreType.DMA((10,)),
        pltpu.SemaphoreType.DMA((2, 2, 3)),
        pltpu.SemaphoreType.DMA((2, 2, 9)),
        pltpu.SemaphoreType.DMA((2, 2, 3)),
        pltpu.SemaphoreType.DMA((2, 2, 9)),
        pltpu.SemaphoreType.DMA((2, 2)),
        pltpu.SemaphoreType.DMA((2, 2)),
        pltpu.SemaphoreType.DMA((1,)),
        pltpu.SemaphoreType.DMA((1,)),
        pltpu.SemaphoreType.DMA((2,)),
        pltpu.SemaphoreType.DMA((2,)),
        pltpu.SemaphoreType.DMA((2, 7)),
        pltpu.SemaphoreType.DMA((2, 7)),
    ]
    for t in range(3):
        full = ORDERS[t][:2]
        scratch.append(pltpu.VMEM((2, 2, 2) + lead_shape(full) + (16, 128), BF))
        for st in range(3):
            full = ORDERS[t][: 2 - st]
            scratch.append(pltpu.VMEM((2, 2, 3 if st else 2) + lead_shape(full) + (16, 256), BF))
    out, app = pl.pallas_call(
        kernel,
        out_shape=(
            jax.ShapeDtypeStruct((2, 4, 3, 16, 1024), BF),
            jax.ShapeDtypeStruct((2, 2, 16, 128), BF),
        ),
        in_specs=[anyspace, vmem, vmem] + [anyspace] * 9 + [smem, smem, vmem],
        out_specs=(anyspace, vmem),
        scratch_shapes=scratch,
        compiler_params=pltpu.CompilerParams(
            collective_id=0, has_side_effects=True, vmem_limit_bytes=63 * 1024 * 1024
        ),
    )(
        embeds.reshape(2, 4, 3, 16, 1024),
        attn_gain,
        ffn_gain,
        query_weight.reshape(8, 2, 1024, 128),
        key_matrix.T,
        value_matrix.T,
        output_weight,
        gate_weight.T,
        up_weight.T,
        down_weight,
        rotated_key_cache.reshape(LOCAL, SLOTS, HEAD),
        stored_value_cache.reshape(LOCAL, SLOTS, HEAD),
        lengths,
        positions,
        freq,
    )
    return pl.pallas_call(
        finish,
        out_shape=(
            jax.ShapeDtypeStruct((2, ROWS, 1024), BF),
            jax.ShapeDtypeStruct((2, LOCAL, 2, HEAD), BF),
        ),
        in_specs=[vmem, vmem],
        out_specs=(vmem, vmem),
    )(out.reshape(2, ROWS, 1024), app)


def solution(mesh):
    in_specs = (
        P(None, None, "col"),
        P("col"),
        P("col"),
        P(None, ("row", "col")),
        P(None, ("row", "col")),
        P(None, ("row", "col")),
        P(("row", "col"), None),
        P(None, ("row", "col")),
        P(None, ("row", "col")),
        P(("row", "col"), None),
        P("col", "row", None, None),
        P("col", "row", None, None),
        P("col"),
        P("col"),
    )
    out_specs = (P(None, None, "col"), P(None, "col", None, "row"))
    return jax.shard_map(on_device, mesh=mesh, in_specs=in_specs, out_specs=out_specs, check_vma=False)
```
